512 devices in a mesh: pool: 16 (over x, z_lo, core), tp: 8 (over y), req: 4 (over z_hi).
Axes of the slice: x: 4, y: 8, z: 8 (z_hi: 4, z_lo: 2; z = z_hi * 2 + z_lo), core: 2. Of those that a mesh axis runs over, the one named last changes fastest.
Arguments:
- hidden_in: bfloat16 [4, 2048, 8192], P('req', 'pool', 'tp'), may hold values from -6 to 6
- base_query_rotated: bfloat16 [4, 2048, 8192], P('req', 'pool', 'tp'), may hold values from -6 to 6
- suffix_cache: bfloat16 [4, 2, 2048, 1024], P('req', None, 'pool', 'tp'), may hold values from -6 to 6
- cache_pool: bfloat16 [320, 2, 128, 1024], P('pool', None, None, 'tp'), may hold values from -6 to 6
- adapter_down: bfloat16 [8, 8192, 16], P(None, 'tp'), may hold values from -0.0625 to 0.0625
- adapter_up: bfloat16 [8, 16, 8192], P(None, None, 'tp'), may hold values from -1.5 to 1.5
- block_table: int32 [4, 32], replicated, may hold values from 0 to 319, as said below
- prefix_lengths: int32 [4], replicated, may hold values from 1024 to 4096, as said below
- suffix_lengths: int32 [4], replicated, may hold values from 512 to 2048, as said below
- tenant_adapter: int32 [4], replicated, may hold values from 0 to 7
- write_slots: int32 [4, 16], replicated, may hold values from 0 to 319, as said below
Outputs:
- attended: bfloat16 [4, 2048, 8192], P('req', 'pool', 'tp')
- pool_after: bfloat16 [320, 2, 128, 1024], P('pool', None, None, 'tp')
The draws below stay inside these ranges and needn't reach their ends.
Inputs may be any that keep to these rules, and one draw needn't show every extreme that they name: All entries of block_table and write_slots together are distinct slots. Slot s lies on pool device s // 20. For each tenant, no pool device holds more than 4 of its prefix blocks, and one holds exactly 4. `write_slots`: for each tenant, every pool device receives exactly 1 of its slots. `prefix_lengths`: some tenant has exactly 4096. `suffix_lengths`: some tenant has exactly 2048.
All inputs are finite; a program needn't handle non-finite values.
Results may differ from the reference program's by a relative error of at most 0.0095.
Values may be sent and summed in bfloat16 or wider, within the bound.
A program may use at most 64 MiB of HBM per device.

```python
import jax
import jax.numpy as jnp
from jax import lax

D = 8192
HEADS = 64
KVH = 8
HD = 128
RANK = 16
ADAPTERS = 8
BLOCK = 128
PBLK = 32
TENANTS = 4
SUF = 2048
SBLK = 16
PREF = 4096
MOST = 4
SLOT_DEV = 20
SLOTS = 320
N_POOL = 16


def pool_layout(key):
    splits = jax.random.split(key, 3)
    local_perm = jax.vmap(lambda sub: jax.random.permutation(sub, SLOT_DEV))(jax.random.split(splits[0], N_POOL))

    def tenant_owners(sub):
        parts = jax.random.split(sub, 3)
        heavy = jax.random.randint(parts[0], (), 0, N_POOL)
        others_perm = jax.random.permutation(parts[1], N_POOL - 1)
        order = jax.random.permutation(parts[2], PBLK)
        is_heavy = order < MOST
        spread = jnp.maximum(order - MOST, 0)
        owners = jnp.where(is_heavy, heavy, (heavy + 1 + others_perm[spread % (N_POOL - 1)]) % N_POOL)
        ranks = jnp.where(is_heavy, order, spread // (N_POOL - 1))
        return (owners, ranks)
    owners, ranks = jax.vmap(tenant_owners)(jax.random.split(splits[1], TENANTS))
    tenant_ids = jnp.arange(TENANTS)[:, None]
    local = local_perm[owners, tenant_ids * MOST + ranks]
    table = owners * SLOT_DEV + local
    flat = jnp.arange(TENANTS * SBLK)
    write_perm = jax.random.permutation(splits[2], N_POOL)
    write_owner = write_perm[flat % N_POOL]
    write_local = local_perm[write_owner, TENANTS * MOST + flat // N_POOL]
    writes = (write_owner * SLOT_DEV + write_local).reshape(TENANTS, SBLK)
    return (table.astype(jnp.int32), writes.astype(jnp.int32))


def draw_block_table(key, part):
    table, writes = pool_layout(key)
    return table


def draw_write_slots(key, part):
    table, writes = pool_layout(key)
    return writes


def draw_prefix_lengths(key, part):
    key = jax.random.fold_in(key, 3)
    first, second = jax.random.split(key)
    lengths = jax.random.randint(first, (TENANTS,), PREF // 4, PREF + 1)
    longest = jax.random.randint(second, (), 0, TENANTS)
    return jnp.where(jnp.arange(TENANTS) == longest, PREF, lengths).astype(jnp.int32)


def draw_suffix_lengths(key, part):
    key = jax.random.fold_in(key, 4)
    first, second = jax.random.split(key)
    lengths = jax.random.randint(first, (TENANTS,), SUF // 4, SUF + 1)
    longest = jax.random.randint(second, (), 0, TENANTS)
    return jnp.where(jnp.arange(TENANTS) == longest, SUF, lengths).astype(jnp.int32)


def draw_base_query_rotated(key, part):
    key = jax.random.fold_in(key, 5)
    first = jax.random.fold_in(key, 0)
    shape = (TENANTS, SUF, HEADS * HD)
    values = jax.random.normal(first, shape, jnp.float32)
    return jnp.clip(values, -6.0, 6.0).astype(jnp.bfloat16)


def draw_suffix_cache(key, part):
    key = jax.random.fold_in(key, 6)
    shape = (TENANTS, 2, SUF, KVH * HD)
    values = jax.random.normal(key, shape, jnp.float32)
    return jnp.clip(values, -6.0, 6.0).astype(jnp.bfloat16)


def with_ends(values, key, least, top_value):
    dims = values.shape
    spot = [jax.random.randint(jax.random.fold_in(key, axis), (), 0, dims[axis]) for axis in range(len(dims))]
    values = values.at[tuple(spot)].set(least)
    longest = dims.index(max(dims))
    spot[longest] = (spot[longest] + 1) % dims[longest]
    return values.at[tuple(spot)].set(top_value)


def steps_of(rng, extent, cuts, low, high):
    def one(dim, blocks):
        heights = jax.random.uniform(jax.random.fold_in(jax.random.fold_in(rng, 6), dim), (blocks,), jnp.float32, low / len(cuts), high / len(cuts))
        return jnp.repeat(jnp.exp(heights), extent[dim] // blocks).reshape((-1,) + (1,) * (len(extent) - dim - 1))

    gain = one(*cuts[0])
    for cut in cuts[1:]:
        gain = gain * one(*cut)
    return gain


def normal_values(stream_key, dims, width, reach, pieces=(), held_as=jnp.bfloat16):
    result = width * jax.random.normal(stream_key, dims, jnp.float32)
    if pieces:
        result = result * steps_of(stream_key, dims, pieces, -0.22, 0.18)
    return jnp.clip(result, -reach, reach).astype(held_as)


def setup_inputs(seed: int = 0) -> dict:
    arg_keys = jax.random.split(jax.random.key(seed), 12)
    return {
        "hidden_in": normal_values(arg_keys[0], (TENANTS, SUF, D), 1.0, 6.0, ((0, 4), (1, 16), (2, 8))),
        "base_query_rotated": draw_base_query_rotated(jax.random.fold_in(arg_keys[11], 71), 0),
        "suffix_cache": draw_suffix_cache(jax.random.fold_in(arg_keys[11], 71), 0),
        "cache_pool": normal_values(arg_keys[3], (SLOTS, 2, BLOCK, KVH * HD), 1.0, 6.0, ((0, 16), (3, 8))),
        "adapter_down": normal_values(arg_keys[4], (ADAPTERS, D, RANK), D ** -0.5, 0.0625, ((1, 8),)),
        "adapter_up": normal_values(arg_keys[5], (ADAPTERS, RANK, HEADS * HD), RANK ** -0.5, 1.5, ((2, 8),)),
        "block_table": draw_block_table(jax.random.fold_in(arg_keys[11], 71), 0),
        "prefix_lengths": draw_prefix_lengths(jax.random.fold_in(arg_keys[11], 71), 0),
        "suffix_lengths": draw_suffix_lengths(jax.random.fold_in(arg_keys[11], 71), 0),
        "tenant_adapter": with_ends(jax.random.randint(arg_keys[9], (TENANTS,), 0, ADAPTERS), jax.random.fold_in(arg_keys[9], 1), 0, ADAPTERS - 1).astype(jnp.int32),
        "write_slots": draw_write_slots(jax.random.fold_in(arg_keys[11], 71), 0),
    }


ADAPTER_SCALING = 0.5


def reference(hidden_in, base_query_rotated, suffix_cache, cache_pool, adapter_down, adapter_up, block_table, prefix_lengths, suffix_lengths, tenant_adapter, write_slots):
    groups = HEADS // KVH
    score_scale = HD ** -0.5
    key_value_width = KVH * HD
    results = []
    for tenant_index in range(TENANTS):
        adapter = tenant_adapter[tenant_index]
        rank_vec = jnp.dot(hidden_in[tenant_index], adapter_down[adapter], preferred_element_type=jnp.float32).astype(jnp.bfloat16)
        low_rank_update = jnp.dot(rank_vec, adapter_up[adapter], preferred_element_type=jnp.float32)
        query_rows_all = (base_query_rotated[tenant_index].astype(jnp.float32) + ADAPTER_SCALING * low_rank_update).astype(jnp.bfloat16)
        prefix = jnp.take(cache_pool, block_table[tenant_index], axis=0)
        key_rows = jnp.concatenate([prefix[:, 0].reshape(PREF, key_value_width), suffix_cache[tenant_index, 0]], axis=0)
        value_rows = jnp.concatenate([prefix[:, 1].reshape(PREF, key_value_width), suffix_cache[tenant_index, 1]], axis=0)
        position = jnp.arange(PREF + SUF, dtype=jnp.int32)
        query_pos = jnp.arange(SUF, dtype=jnp.int32)
        visible = jnp.where(position[None, :] < PREF, position[None, :] < prefix_lengths[tenant_index], (position[None, :] - PREF) <= query_pos[:, None])
        query_heads = query_rows_all.astype(jnp.float32).reshape(SUF, KVH, groups, HD).transpose(1, 2, 0, 3)
        key_heads = key_rows.astype(jnp.float32).reshape(PREF + SUF, KVH, HD).transpose(1, 0, 2)
        value_heads = value_rows.astype(jnp.float32).reshape(PREF + SUF, KVH, HD).transpose(1, 0, 2)

        def one_head(member):
            query_set, key_set, value_set = member
            scores = jnp.einsum('grd,ld->grl', query_set, key_set) * score_scale
            masked = jnp.where(visible[None], scores, -1e30)
            row_peak = jnp.max(masked, axis=-1, keepdims=True)
            weights = jnp.where(visible[None], jnp.exp(scores - row_peak), 0.0)
            row_total = jnp.sum(weights, axis=-1, keepdims=True)
            rounded = weights.astype(jnp.bfloat16).astype(jnp.float32)
            return jnp.einsum('grl,ld->grd', rounded, value_set) / row_total

        heads_out = lax.map(one_head, (query_heads, key_heads, value_heads))
        merged = heads_out.transpose(2, 0, 1, 3).reshape(SUF, HEADS * HD)
        merged = jnp.where((query_pos < suffix_lengths[tenant_index])[:, None], merged, 0.0)
        results.append(merged.astype(jnp.bfloat16))
    attended = jnp.stack(results, axis=0)
    blocks_all = suffix_cache.reshape(TENANTS, 2, SBLK, BLOCK, key_value_width).transpose(0, 2, 1, 3, 4).reshape(TENANTS * SBLK, 2, BLOCK, key_value_width)
    pool_after = cache_pool.at[write_slots.reshape(-1)].set(blocks_all)
    return attended, pool_after
```

```python
import functools

import jax
import jax.numpy as jnp
from jax import lax
from jax.experimental import pallas as pl
from jax.experimental.pallas import tpu as pltpu
from jax.sharding import PartitionSpec as P

MESH = pl.DeviceIdType.MESH
HD = 128
ADAPTER_SCALING = 0.5
LOG2E = 1.4426950408889634
LOW = -1e30
ROWS = 256
PARTNERS = ("sib", "xp", "xm", "zp", "zn", "y1", "y2", "y4", "rp", "rm")
COPIES = 46


def kernel(
    table, plens, slens, adapters, wslots,
    hidden, base, suffix, pool, down, up,
    out, pool_out,
    pool_v, hid_v, base_v, down_v, up_v,
    main_0, main_1, main_2, main_3, over_0, over_1, over_2, over_3, cont_0, cont_1, cont_2, cont_3,
    fore, wblk, wmine,
    rank_out, rank_in, qs, peak, acc, kc, vc, nval,
    local_sem, send_sem, recv_sem,
):
    p = lax.axis_index("pool")
    y = lax.axis_index("tp")
    r = lax.axis_index("req")
    x, zl, c = p // 4, (p // 2) % 2, p % 2
    x1, x3 = (x + 1) % 4, (x + 3) % 4
    rn = (r + 2 * zl + 3) % 4
    other = p + 2 - 4 * zl
    partner = {
        "sib": {"pool": p + 1 - 2 * c},
        "xp": {"pool": x1 * 4 + zl * 2 + c},
        "xm": {"pool": x3 * 4 + zl * 2 + c},
        "zp": {"pool": other},
        "zn": {"pool": other, "req": rn},
        "y1": {"tp": y + 1 - 2 * (y % 2)},
        "y2": {"tp": y + 2 - 4 * ((y // 2) % 2)},
        "y4": {"tp": (y + 4) % 8},
        "rp": {"req": (r + 1) % 4},
        "rm": {"req": (r + 3) % 4},
    }

    main = (main_0, main_1, main_2, main_3)
    over = (over_0, over_1, over_2, over_3)
    cont = (cont_0, cont_1, cont_2, cont_3)

    def device_of(k, i, j):
        return (x + k) % 4 * 4 + (zl + j - 2 * zl * j) * 2 + c + i - 2 * c * i

    locals_ = {}
    for i, (name, src, dst) in enumerate((
        ("suffix", suffix.at[0], cont_0.at[0, 0]),
        ("pool", pool, pool_v),
        ("hidden", hidden.at[0], hid_v),
        ("down", down, down_v),
        ("base", base.at[0], base_v),
        ("up", up, up_v),
    )):
        locals_[name] = pltpu.make_async_copy(src, dst, local_sem.at[i])
        locals_[name].start()

    barrier = pltpu.get_barrier_semaphore()
    for name in PARTNERS:
        pl.semaphore_signal(barrier, inc=1, device_id=partner[name], device_id_type=MESH)
    pl.semaphore_wait(barrier, len(PARTNERS))

    copies = {}

    def send_to(name, src, dst, to):
        i = len(copies)
        copy = pltpu.make_async_remote_copy(
            src_ref=src, dst_ref=dst,
            send_sem=send_sem.at[i], recv_sem=recv_sem.at[i],
            device_id=partner[to], device_id_type=MESH,
        )
        copies[name] = copy
        copy.start()

    def send(name, buf, k, at, to):
        there = (k + {"xp": 3, "xm": 1}.get(to, 0)) % 4
        place = list(at)
        if to == "sib":
            place[0] = 1 - at[0]
        if to in ("zp", "zn"):
            place[1] = 1 - at[1]
        send_to(name, buf[k].at[at], buf[there].at[tuple(place)], to)

    def got(*names):
        for name in names:
            copies[name].wait_recv()

    locals_["suffix"].wait()
    send("c_z", cont, 0, (0, 0), "zp")

    def own_slots(tenant):
        def step(b, carry):
            count, picks = carry
            local = table[tenant, b] - p * 20
            owned = (local >= 0) & (local < 20)
            picks = tuple(
                jnp.where(owned & (count == k), local, pick) for k, pick in enumerate(picks)
            )
            return count + owned.astype(jnp.int32), picks

        zero = jnp.int32(0)
        return lax.fori_loop(0, 32, step, (zero, (zero,) * 4), unroll=4)[1]

    mine = own_slots(r)
    theirs = own_slots(rn)
    locals_["pool"].wait()
    for k in range(2):
        main_0[0, 0, k] = pool_v[mine[k]]
    send("m_p", main, 0, (0, 0), "xp")
    send("m_m", main, 0, (0, 0), "xm")
    for k in range(2):
        over_0[0, 0, k] = pool_v[mine[2 + k]]
    fore[...] = pool_v[theirs[3]]
    send("o_z", over, 0, (0, 0, 0), "zp")
    send_to("o_n", fore, over_0.at[0, 1, 1], "zn")
    send("m_z", main, 0, (0, 0), "zp")
    send("m_s", main, 0, (0, 0), "sib")

    locals_["hidden"].wait()
    locals_["down"].wait()
    adapter = adapters[r]
    total = lax.dot_general(
        down_v[adapter], hid_v[...], (((1,), (1,)), ((), ())), preferred_element_type=jnp.float32
    )
    rank_out[0] = total
    send_to("r_0", rank_out.at[0], rank_in.at[0], "y1")

    got("c_z")
    send("c_p", cont, 0, (0,), "xp")
    send("c_m", cont, 0, (0,), "xm")
    send("c_s", cont, 0, (0,), "sib")

    plen = plens[r]

    def one_device(d, unused):
        def step(b, carry):
            count, rows = carry
            local = table[r, b] - d * 20
            owned = (local >= 0) & (local < 20)
            seen = plen - b * 128
            rows = tuple(
                jnp.where(owned & (count == k), seen, row) for k, row in enumerate(rows)
            )
            return count + owned.astype(jnp.int32), rows

        zero = jnp.int32(0)
        rows = lax.fori_loop(0, 32, step, (zero, (zero,) * 4), unroll=4)[1]
        for k in range(4):
            nval[d * 4 + k] = rows[k]
        return unused

    lax.fori_loop(0, 16, one_device, 0)

    got("r_0")
    total = total + rank_in[0]
    rank_out[1] = total
    send_to("r_1", rank_out.at[1], rank_in.at[1], "y2")
    got("o_z", "o_n")
    send("o_p", over, 0, (0,), "xp")
    send("o_m", over, 0, (0,), "xm")
    send("o_s", over, 0, (0,), "sib")
    got("r_1")
    total = total + rank_in[1]
    rank_out[2] = total
    send_to("r_2", rank_out.at[2], rank_in.at[2], "y4")
    got("m_p")
    send("m_pp", main, 3, (0, 0, 0), "xp")
    send("m_pz", main, 3, (0, 0), "zp")
    send("m_ps", main, 3, (0, 0), "sib")
    got("m_m")
    send("m_mm", main, 1, (0, 0, 1), "xm")
    send("m_mz", main, 1, (0, 0), "zp")
    send("m_ms", main, 1, (0, 0), "sib")
    got("r_2")
    total = total + rank_in[2]
    rank = total.T.astype(jnp.bfloat16)
    locals_["base"].wait()
    locals_["up"].wait()
    update = jnp.dot(rank, up_v[adapter], preferred_element_type=jnp.float32)
    query = (base_v[...].astype(jnp.float32) + ADAPTER_SCALING * update).astype(jnp.bfloat16)
    for h in range(8):
        qs[h * 128 : (h + 1) * 128, :] = query[:, h * 128 : (h + 1) * 128]

    peak[...] = jnp.full(peak.shape, LOW, jnp.float32)
    acc[...] = jnp.zeros(acc.shape, jnp.float32)
    scale = HD**-0.5 * LOG2E
    own_key = cont_0[0, 0, 0, 0:1, :]

    def attend(mask):
        keys = kc[...]
        values = vc[...]
        for t in range(1024 // ROWS):
            rows = slice(t * ROWS, (t + 1) * ROWS)
            s = lax.dot_general(
                qs[rows, :], keys, (((1,), (1,)), ((), ())), preferred_element_type=jnp.float32
            )
            if mask is not None:
                s = jnp.where(mask, s, LOW)
            old = peak[rows, 0:1]
            new = jnp.maximum(old, jnp.max(s, axis=1, keepdims=True))
            w = jnp.exp2((s - new) * scale).astype(jnp.bfloat16)
            factor = jnp.exp2((old - new) * scale)
            acc[rows, :] = acc[rows, :] * factor + jnp.dot(
                w, values, preferred_element_type=jnp.float32
            )
            peak[rows, :] = jnp.broadcast_to(new, (ROWS, 128))

    def suffix_plane(k, mask):
        for i in range(4):
            at = slice(i * 128, (i + 1) * 128)
            kc[at, :] = cont[k][i % 2, i // 2, 0]
            vc[at, :128] = cont[k][i % 2, i // 2, 1]
            vc[at, 128:] = jnp.ones((128, 128), jnp.bfloat16)
        attend(mask)

    row_no = lax.broadcasted_iota(jnp.int32, (128, 128), 0)

    def prefix_plane(buf, k, first):
        def one(i, unused):
            for n in range(4):
                at = slice(n * 128, (n + 1) * 128)
                j, slot = n // 2, n % 2
                seen = row_no < nval[device_of(k, i, j) * 4 + first + slot]
                kc[at, :] = jnp.where(seen, buf[k][i, j, slot, 0], own_key)
                vc[at, :128] = jnp.where(seen, buf[k][i, j, slot, 1], jnp.bfloat16(0))
                vc[at, 128:] = jnp.where(seen, jnp.bfloat16(1), jnp.bfloat16(0))
            attend(None)
            return unused

        lax.fori_loop(0, 2, one, 0)

    got("c_s")
    lane = lax.broadcasted_iota(jnp.int32, (ROWS, 128), 1)
    token = lax.broadcasted_iota(jnp.int32, (ROWS, 128), 0) % 128 + p * 128
    suffix_plane(0, jnp.concatenate(
        [lane + device_of(0, i % 2, i // 2) * 128 <= token for i in range(4)], axis=1
    ))

    got("m_z", "m_s")
    send("m_zs", main, 0, (0, 1), "sib")
    got("m_pz", "m_mz")
    send("m_pzs", main, 3, (0, 1), "sib")
    send("m_mzs", main, 1, (0, 1), "sib")
    got("m_pp")
    send("m_ppz", main, 2, (0, 0, 0), "zp")
    send("m_pps", main, 2, (0, 0, 0), "sib")
    got("m_mm")
    send("m_mmz", main, 2, (0, 0, 1), "zp")
    send("m_mms", main, 2, (0, 0, 1), "sib")
    got("c_p")
    send("c_pp", cont, 3, (0, 0), "xp")
    send("c_ps", cont, 3, (0,), "sib")
    got("c_m")
    send("c_mm", cont, 1, (0, 1), "xm")
    send("c_ms", cont, 1, (0,), "sib")
    got("m_zs")
    prefix_plane(main, 0, 0)

    got("o_p")
    send("o_pp", over, 3, (0, 0), "xp")
    send("o_ps", over, 3, (0,), "sib")
    got("o_m")
    send("o_mm", over, 1, (0, 1), "xm")
    send("o_ms", over, 1, (0,), "sib")
    got("c_pp")
    send("c_pps", cont, 2, (0, 0), "sib")
    got("c_mm")
    send("c_mms", cont, 2, (0, 1), "sib")
    got("m_ppz", "m_mmz")
    send("m_zzs", main, 2, (0, 1), "sib")

    got("m_ps", "m_pzs")
    prefix_plane(main, 3, 0)
    got("m_ms", "m_mzs")
    prefix_plane(main, 1, 0)

    got("c_ps", "c_ms", "c_pps", "c_mms")

    def write_slot(tenant):
        def step(b, carry):
            block, slot = carry
            local = wslots[tenant, b] - p * 20
            owned = (local >= 0) & (local < 20)
            return jnp.where(owned, b, block), jnp.where(owned, local, slot)

        return lax.fori_loop(0, 16, step, (jnp.int32(0), jnp.int32(0)), unroll=4)

    block, slot_0 = write_slot(r)
    i, j = (block + c) % 2, (block // 2 + zl) % 2
    away = (block // 4 + 4 - x) % 4
    chosen = cont_0[i, j]
    for k in range(1, 4):
        chosen = jnp.where(away == k, cont[k][i, j], chosen)
    wmine[...] = chosen
    send_to("w_p", wmine, wblk.at[2], "rp")
    send_to("w_m", wmine, wblk.at[0], "rm")

    for k in range(1, 4):
        pl.when(x + k >= 4)(functools.partial(suffix_plane, k, None))
    got("o_s")
    prefix_plane(over, 0, 2)

    got("o_pp")
    send("o_pps", over, 2, (0, 0), "sib")
    got("o_mm")
    send("o_mms", over, 2, (0, 1), "sib")
    got("w_p")
    send_to("w_pp", wblk.at[2, 0], wblk.at[1, 0], "rp")
    got("w_m")
    send_to("w_mm", wblk.at[0, 1], wblk.at[1, 1], "rm")

    got("m_pps", "m_mms", "m_zzs")
    prefix_plane(main, 2, 0)
    got("o_ps")
    prefix_plane(over, 3, 2)
    got("o_ms")
    prefix_plane(over, 1, 2)
    got("o_pps", "o_mms")
    prefix_plane(over, 2, 2)

    slot_1 = write_slot((r + 1) % 4)[1]
    slot_2 = write_slot((r + 2) % 4)[1]
    slot_3 = write_slot((r + 3) % 4)[1]
    got("w_pp", "w_mm")

    def one_slot(s, unused):
        block = pool_v[s]
        block = jnp.where(s == slot_0, wmine[...], block)
        block = jnp.where(s == slot_1, wblk[0], block)
        block = jnp.where(s == slot_2, wblk[1], block)
        block = jnp.where(s == slot_3, wblk[2], block)
        pool_out[s] = block
        return unused

    lax.fori_loop(0, 20, one_slot, 0)

    token = p * 128 + lax.broadcasted_iota(jnp.int32, (128, 128), 0)
    live = token < slens[r]
    for h in range(8):
        rows = slice(h * 128, (h + 1) * 128)
        value = acc[rows, :128] / acc[rows, 128:]
        out[0, :, rows] = jnp.where(live, value, 0.0).astype(jnp.bfloat16)

    for copy in copies.values():
        copy.wait_send()


def local(hidden, base, suffix, pool, down, up, table, plens, slens, adapters, wslots):
    bf, f32 = jnp.bfloat16, jnp.float32
    down = down.transpose(0, 2, 1)
    smem = pl.BlockSpec(memory_space=pltpu.SMEM)
    anywhere = pl.BlockSpec(memory_space=pl.ANY)
    vmem = pl.BlockSpec(memory_space=pltpu.VMEM)
    block = (2, 128, 128)
    return pl.pallas_call(
        kernel,
        out_shape=(
            jax.ShapeDtypeStruct(base.shape, bf),
            jax.ShapeDtypeStruct(pool.shape, bf),
        ),
        in_specs=[smem] * 5 + [anywhere] * 6,
        out_specs=(vmem, vmem),
        scratch_shapes=[
            pltpu.VMEM(pool.shape, bf),
            pltpu.VMEM(hidden.shape[1:], bf),
            pltpu.VMEM(base.shape[1:], bf),
            pltpu.VMEM(down.shape, bf),
            pltpu.VMEM(up.shape, bf),
            *[pltpu.VMEM((2, 2, 2) + block, bf)] * 8,
            *[pltpu.VMEM((2, 2) + block, bf)] * 4,
            pltpu.VMEM(block, bf),
            pltpu.VMEM((3,) + block, bf),
            pltpu.VMEM(block, bf),
            pltpu.VMEM((3, 16, 128), f32),
            pltpu.VMEM((3, 16, 128), f32),
            pltpu.VMEM((1024, 128), bf),
            pltpu.VMEM((1024, 128), f32),
            pltpu.VMEM((1024, 256), f32),
            pltpu.VMEM((512, 128), bf),
            pltpu.VMEM((512, 256), bf),
            pltpu.SMEM((64,), jnp.int32),
            pltpu.SemaphoreType.DMA((6,)),
            pltpu.SemaphoreType.DMA((COPIES,)),
            pltpu.SemaphoreType.DMA((COPIES,)),
        ],
        compiler_params=pltpu.CompilerParams(
            collective_id=0, has_side_effects=True, vmem_limit_bytes=48 << 20
        ),
        name="attend_all",
    )(table, plens, slens, adapters, wslots, hidden, base, suffix, pool, down, up)


def solution(mesh):
    in_specs = (
        P("req", "pool", "tp"),
        P("req", "pool", "tp"),
        P("req", None, "pool", "tp"),
        P("pool", None, None, "tp"),
        P(None, "tp", None),
        P(None, None, "tp"),
        P(),
        P(),
        P(),
        P(),
        P(),
    )
    out_specs = (P("req", "pool", "tp"), P("pool", None, None, "tp"))
    return jax.shard_map(local, mesh=mesh, in_specs=in_specs, out_specs=out_specs, check_vma=False)
```

```python
import functools

import jax
import jax.numpy as jnp
from jax import lax
from jax.experimental import pallas as pl
from jax.experimental.pallas import tpu as pltpu
from jax.sharding import PartitionSpec as P

MESH = pl.DeviceIdType.MESH
HD = 128
ADAPTER_SCALING = 0.5
LOG2E = 1.4426950408889634
LOW = -1e30
ROWS = 128
PARTNERS = ("sib", "xp", "xm", "zp", "zn", "y1", "y2", "y3", "y4", "y5", "y6", "y7", "rp", "rm")
COPIES = 50


def kernel(
    table_in, plens_in, slens_in, adapters_in, wslots_in,
    hidden, base, suffix, pool, down, up,
    out, pool_out,
    table, plens, slens, adapters, wslots,
    pool_v, hid_v, base_v, down_v, up_v,
    main_0, main_1, main_2, main_3, over_0, over_1, over_2, over_3, cont_0, cont_1, cont_2, cont_3,
    fore, wblk, wmine,
    rank_out, rank_in, qs, peak, acc, kc, vc, nval,
    local_sem, send_sem, recv_sem,
):
    p = lax.axis_index("pool")
    y = lax.axis_index("tp")
    r = lax.axis_index("req")
    x, zl, c = p // 4, (p // 2) % 2, p % 2
    x1, x3 = (x + 1) % 4, (x + 3) % 4
    rn = (r + 2 * zl + 3) % 4
    other = p + 2 - 4 * zl
    partner = {
        "sib": {"pool": p + 1 - 2 * c},
        "xp": {"pool": x1 * 4 + zl * 2 + c},
        "xm": {"pool": x3 * 4 + zl * 2 + c},
        "zp": {"pool": other},
        "zn": {"pool": other, "req": rn},
        **{f"y{d}": {"tp": (y + d) % 8} for d in range(1, 8)},
        "rp": {"req": (r + 1) % 4},
        "rm": {"req": (r + 3) % 4},
    }

    main = (main_0, main_1, main_2, main_3)
    over = (over_0, over_1, over_2, over_3)
    cont = (cont_0, cont_1, cont_2, cont_3)

    def device_of(k, i, j):
        return (x + k) % 4 * 4 + (zl + j - 2 * zl * j) * 2 + c + i - 2 * c * i

    locals_ = {}
    for i, (name, src, dst) in enumerate((
        ("table", table_in, table),
        ("suffix", suffix.at[0], cont_0.at[0, 0]),
        ("pool", pool, pool_v),
        ("adapters", adapters_in, adapters),
        ("hidden", hidden.at[0], hid_v),
        ("down", down, down_v),
        ("base", base.at[0], base_v),
        ("up", up, up_v),
        ("plens", plens_in, plens),
        ("slens", slens_in, slens),
        ("wslots", wslots_in, wslots),
    )):
        locals_[name] = pltpu.make_async_copy(src, dst, local_sem.at[i])
        locals_[name].start()

    barrier = pltpu.get_barrier_semaphore()
    for name in PARTNERS:
        pl.semaphore_signal(barrier, inc=1, device_id=partner[name], device_id_type=MESH)
    pl.semaphore_wait(barrier, len(PARTNERS))

    copies = {}

    def send_to(name, src, dst, to):
        i = len(copies)
        copy = pltpu.make_async_remote_copy(
            src_ref=src, dst_ref=dst,
            send_sem=send_sem.at[i], recv_sem=recv_sem.at[i],
            device_id=partner[to], device_id_type=MESH,
        )
        copies[name] = copy
        copy.start()

    def send(name, buf, k, at, to):
        there = (k + {"xp": 3, "xm": 1}.get(to, 0)) % 4
        place = list(at)
        if to == "sib":
            place[0] = 1 - at[0]
        if to in ("zp", "zn"):
            place[1] = 1 - at[1]
        send_to(name, buf[k].at[at], buf[there].at[tuple(place)], to)

    def got(*names):
        for name in names:
            copies[name].wait_recv()

    locals_["suffix"].wait()
    send("c_z", cont, 0, (0, 0), "zp")

    def own_slots(tenant):
        def step(b, carry):
            count, picks = carry
            local = table[tenant, b] - p * 20
            owned = (local >= 0) & (local < 20)
            picks = tuple(
                jnp.where(owned & (count == k), local, pick) for k, pick in enumerate(picks)
            )
            return count + owned.astype(jnp.int32), picks

        zero = jnp.int32(0)
        return lax.fori_loop(0, 32, step, (zero, (zero,) * 4), unroll=4)[1]

    locals_["table"].wait()
    mine = own_slots(r)
    locals_["pool"].wait()
    for k in range(2):
        main_0[0, 0, k] = pool_v[mine[k]]
    send("m_p", main, 0, (0, 0), "xp")
    send("m_m", main, 0, (0, 0), "xm")
    send("m_z", main, 0, (0, 0), "zp")

    locals_["hidden"].wait()
    locals_["down"].wait()
    locals_["adapters"].wait()
    adapter = adapters[r]
    rank_out[...] = lax.dot_general(
        down_v[adapter], hid_v[...], (((1,), (1,)), ((), ())), preferred_element_type=jnp.float32
    )
    for d in range(1, 8):
        send_to(f"r_{d}", rank_out, rank_in.at[8 - d], f"y{d}")

    theirs = own_slots(rn)
    for k in range(2):
        over_0[0, 0, k] = pool_v[mine[2 + k]]
    fore[...] = pool_v[theirs[3]]
    send("o_z", over, 0, (0, 0, 0), "zp")
    send_to("o_n", fore, over_0.at[0, 1, 1], "zn")
    send("m_s", main, 0, (0, 0), "sib")

    got("c_z")
    send("c_p", cont, 0, (0,), "xp")
    send("c_m", cont, 0, (0,), "xm")
    send("c_s", cont, 0, (0,), "sib")

    locals_["plens"].wait()
    plen = plens[r]

    def one_device(d, unused):
        def step(b, carry):
            count, rows = carry
            local = table[r, b] - d * 20
            owned = (local >= 0) & (local < 20)
            seen = plen - b * 128
            rows = tuple(
                jnp.where(owned & (count == k), seen, row) for k, row in enumerate(rows)
            )
            return count + owned.astype(jnp.int32), rows

        zero = jnp.int32(0)
        rows = lax.fori_loop(0, 32, step, (zero, (zero,) * 4), unroll=4)[1]
        for k in range(4):
            nval[d * 4 + k] = rows[k]
        return unused

    lax.fori_loop(0, 16, one_device, 0)

    got("o_z", "o_n")
    send("o_p", over, 0, (0,), "xp")
    send("o_m", over, 0, (0,), "xm")
    send("o_s", over, 0, (0,), "sib")
    got("m_p")
    send("m_pp", main, 3, (0, 0, 0), "xp")
    send("m_pz", main, 3, (0, 0), "zp")
    send("m_ps", main, 3, (0, 0), "sib")
    got("m_m")
    send("m_mm", main, 1, (0, 0, 1), "xm")
    send("m_mz", main, 1, (0, 0), "zp")
    send("m_ms", main, 1, (0, 0), "sib")
    got(*(f"r_{d}" for d in range(1, 8)))
    total = rank_out[...]
    for d in range(1, 8):
        total = total + rank_in[d]
    rank = total.T.astype(jnp.bfloat16)
    locals_["base"].wait()
    locals_["up"].wait()
    update = jnp.dot(rank, up_v[adapter], preferred_element_type=jnp.float32)
    query = (base_v[...].astype(jnp.float32) + ADAPTER_SCALING * update).astype(jnp.bfloat16)
    for h in range(8):
        qs[h * 128 : (h + 1) * 128, :] = query[:, h * 128 : (h + 1) * 128]

    peak[...] = jnp.full(peak.shape, LOW, jnp.float32)
    acc[...] = jnp.zeros(acc.shape, jnp.float32)
    scale = HD**-0.5 * LOG2E
    own_key = cont_0[0, 0, 0, 0:1, :]

    row_no = lax.broadcasted_iota(jnp.int32, (128, 128), 0)

    def fill(n, block, rows):
        at = slice(n * 128, (n + 1) * 128)
        seen = row_no < rows
        kc[at, :] = jnp.where(seen, block[0], own_key)
        vc[at, :128] = jnp.where(seen, block[1], jnp.bfloat16(0))
        vc[at, 128:] = jnp.where(seen, jnp.bfloat16(1), jnp.bfloat16(0))

    def attend(size, mask=None):
        keys = kc[:size, :]
        values = vc[:size, :]

        def scores(t):
            rows = slice(t * ROWS, (t + 1) * ROWS)
            s = lax.dot_general(
                qs[rows, :], keys, (((1,), (1,)), ((), ())), preferred_element_type=jnp.float32
            )
            if mask is not None:
                s = jnp.concatenate([s[:, :-512], jnp.where(mask, s[:, -512:], LOW)], axis=1)
            return s

        later = scores(0)
        for t in range(1024 // ROWS):
            rows = slice(t * ROWS, (t + 1) * ROWS)
            s = later
            if t + 1 < 1024 // ROWS:
                later = scores(t + 1)
            old = peak[rows, 0:1]
            new = jnp.maximum(old, jnp.max(s, axis=1, keepdims=True))
            w = jnp.exp2((s - new) * scale).astype(jnp.bfloat16)
            factor = jnp.exp2((old - new) * scale)
            acc[rows, :] = acc[rows, :] * factor + jnp.dot(
                w, values, preferred_element_type=jnp.float32
            )
            peak[rows, :] = jnp.broadcast_to(new, (ROWS, 128))

    def slots(buf, k, first):
        for n in range(8):
            i, j, slot = n // 4, n // 2 % 2, n % 2
            fill(n, buf[k][i, j, slot], nval[device_of(k, i, j) * 4 + first + slot])

    def plane(k):
        slots(main, k, 0)
        for n in range(4):
            fill(8 + n, cont[k][n // 2, n % 2], 128 if k == 0 else jnp.where(x + k >= 4, 128, 0))
        mask = None
        if k == 0:
            lane = lax.broadcasted_iota(jnp.int32, (ROWS, 128), 1)
            token = lax.broadcasted_iota(jnp.int32, (ROWS, 128), 0) + p * 128
            mask = jnp.concatenate(
                [lane + device_of(0, n // 2, n % 2) * 128 <= token for n in range(4)], axis=1
            )
        attend(1536, mask)

    def over_plane(k):
        slots(over, k, 2)
        attend(1024)

    got("m_z", "m_s")
    send("m_zs", main, 0, (0, 1), "sib")
    got("c_s", "m_zs")
    plane(0)

    got("c_p")
    send("c_pp", cont, 3, (0, 0), "xp")
    send("c_ps", cont, 3, (0,), "sib")
    got("c_m")
    send("c_mm", cont, 1, (0, 1), "xm")
    send("c_ms", cont, 1, (0,), "sib")
    got("m_pz", "m_mz")
    send("m_pzs", main, 3, (0, 1), "sib")
    send("m_mzs", main, 1, (0, 1), "sib")
    got("m_pp")
    send("m_ppz", main, 2, (0, 0, 0), "zp")
    send("m_pps", main, 2, (0, 0, 0), "sib")
    got("m_mm")
    send("m_mmz", main, 2, (0, 0, 1), "zp")
    send("m_mms", main, 2, (0, 0, 1), "sib")
    got("m_ps", "m_pzs", "c_ps")
    plane(3)

    got("c_pp")
    send("c_pps", cont, 2, (0, 0), "sib")
    got("c_mm")
    send("c_mms", cont, 2, (0, 1), "sib")
    got("m_ppz", "m_mmz")
    send("m_zzs", main, 2, (0, 1), "sib")
    got("m_ms", "m_mzs", "c_ms")
    plane(1)

    got("o_p")
    send("o_pp", over, 3, (0, 0), "xp")
    send("o_ps", over, 3, (0,), "sib")
    got("o_m")
    send("o_mm", over, 1, (0, 1), "xm")
    send("o_ms", over, 1, (0,), "sib")
    got("c_pps", "c_mms")

    def write_slot(tenant):
        def step(b, carry):
            block, slot = carry
            local = wslots[tenant, b] - p * 20
            owned = (local >= 0) & (local < 20)
            return jnp.where(owned, b, block), jnp.where(owned, local, slot)

        return lax.fori_loop(0, 16, step, (jnp.int32(0), jnp.int32(0)), unroll=4)

    locals_["wslots"].wait()
    block, slot_0 = write_slot(r)
    i, j = (block + c) % 2, (block // 2 + zl) % 2
    away = (block // 4 + 4 - x) % 4
    chosen = cont_0[i, j]
    for k in range(1, 4):
        chosen = jnp.where(away == k, cont[k][i, j], chosen)
    wmine[...] = chosen
    send_to("w_p", wmine, wblk.at[2], "rp")
    send_to("w_m", wmine, wblk.at[0], "rm")

    got("m_pps", "m_mms", "m_zzs")
    plane(2)
    got("o_pp")
    send("o_pps", over, 2, (0, 0), "sib")
    got("o_mm")
    send("o_mms", over, 2, (0, 1), "sib")
    got("w_p")
    send_to("w_pp", wblk.at[2, 0], wblk.at[1, 0], "rp")
    got("w_m")
    send_to("w_mm", wblk.at[0, 1], wblk.at[1, 1], "rm")
    got("o_s")
    over_plane(0)
    got("o_ps")
    over_plane(3)
    got("o_ms")
    over_plane(1)
    got("o_pps", "o_mms")
    over_plane(2)

    slot_1 = write_slot((r + 1) % 4)[1]
    slot_2 = write_slot((r + 2) % 4)[1]
    slot_3 = write_slot((r + 3) % 4)[1]
    got("w_pp", "w_mm")

    def one_slot(s, unused):
        block = pool_v[s]
        block = jnp.where(s == slot_0, wmine[...], block)
        block = jnp.where(s == slot_1, wblk[0], block)
        block = jnp.where(s == slot_2, wblk[1], block)
        block = jnp.where(s == slot_3, wblk[2], block)
        pool_out[s] = block
        return unused

    lax.fori_loop(0, 20, one_slot, 0)

    token = p * 128 + lax.broadcasted_iota(jnp.int32, (128, 128), 0)
    locals_["slens"].wait()
    live = token < slens[r]
    for h in range(8):
        rows = slice(h * 128, (h + 1) * 128)
        value = acc[rows, :128] / acc[rows, 128:]
        out[0, :, rows] = jnp.where(live, value, 0.0).astype(jnp.bfloat16)

    for copy in copies.values():
        copy.wait_send()


def local(hidden, base, suffix, pool, down, up, table, plens, slens, adapters, wslots):
    bf, f32 = jnp.bfloat16, jnp.float32
    down = down.transpose(0, 2, 1)
    hbm = pl.BlockSpec(memory_space=pltpu.HBM)
    vmem = pl.BlockSpec(memory_space=pltpu.VMEM)
    block = (2, 128, 128)
    return pl.pallas_call(
        kernel,
        out_shape=(
            jax.ShapeDtypeStruct(base.shape, bf),
            jax.ShapeDtypeStruct(pool.shape, bf),
        ),
        in_specs=[hbm] * 11,
        out_specs=(vmem, vmem),
        scratch_shapes=[
            *[pltpu.SMEM(a.shape, jnp.int32) for a in (table, plens, slens, adapters, wslots)],
            pltpu.VMEM(pool.shape, bf),
            pltpu.VMEM(hidden.shape[1:], bf),
            pltpu.VMEM(base.shape[1:], bf),
            pltpu.VMEM(down.shape, bf),
            pltpu.VMEM(up.shape, bf),
            *[pltpu.VMEM((2, 2, 2) + block, bf)] * 8,
            *[pltpu.VMEM((2, 2) + block, bf)] * 4,
            pltpu.VMEM(block, bf),
            pltpu.VMEM((3,) + block, bf),
            pltpu.VMEM(block, bf),
            pltpu.VMEM((16, 128), f32),
            pltpu.VMEM((8, 16, 128), f32),
            pltpu.VMEM((1024, 128), bf),
            pltpu.VMEM((1024, 128), f32),
            pltpu.VMEM((1024, 256), f32),
            pltpu.VMEM((1536, 128), bf),
            pltpu.VMEM((1536, 256), bf),
            pltpu.SMEM((64,), jnp.int32),
            pltpu.SemaphoreType.DMA((11,)),
            pltpu.SemaphoreType.DMA((COPIES,)),
            pltpu.SemaphoreType.DMA((COPIES,)),
        ],
        compiler_params=pltpu.CompilerParams(
            collective_id=0, has_side_effects=True, vmem_limit_bytes=62 << 20
        ),
        name="attend_all",
    )(table, plens, slens, adapters, wslots, hidden, base, suffix, pool, down, up)


def solution(mesh):
    in_specs = (
        P("req", "pool", "tp"),
        P("req", "pool", "tp"),
        P("req", None, "pool", "tp"),
        P("pool", None, None, "tp"),
        P(None, "tp", None),
        P(None, None, "tp"),
        P(),
        P(),
        P(),
        P(),
        P(),
    )
    out_specs = (P("req", "pool", "tp"), P("pool", None, None, "tp"))
    return jax.shard_map(local, mesh=mesh, in_specs=in_specs, out_specs=out_specs, check_vma=False)
```

```python
import functools

import jax
import jax.numpy as jnp
from jax import lax
from jax.experimental import pallas as pl
from jax.experimental.pallas import tpu as pltpu
from jax.sharding import PartitionSpec as P

MESH = pl.DeviceIdType.MESH
HD = 128
ADAPTER_SCALING = 0.5
LOG2E = 1.4426950408889634
LOW = -1e30
ROWS = 128
NEAR = ("sib", "xp", "xm", "zp")
ALONG_TP = (0, 1, 7, 2, 6, 3, 5, 4)
COPIES = 38


def kernel(
    table_in, plens_in, slens_in, adapters_in, wslots_in,
    hidden, base, suffix, pool, down, up,
    out, writes,
    table, plens, slens, adapters, wslots,
    pool_v, hid_v, base_v, down_v, up_v,
    main_0, main_1, main_2, main_3, over_0, over_1, over_2, over_3, cont_0, cont_1, cont_2, cont_3,
    wblk, wmine,
    rank_out, rank_in, qs, peak, acc, kc, vc, nval,
    local_sem, send_sem, recv_sem, rank_ssem, rank_rsem, write_ssem, write_rsem, here_tp, here_req,
):
    p = lax.axis_index("pool")
    y = lax.axis_index("tp")
    r = lax.axis_index("req")
    x, zl, c = p // 4, (p // 2) % 2, p % 2
    x1, x3 = (x + 1) % 4, (x + 3) % 4
    q = jnp.where(y == 0, 0, jnp.where(y <= 4, 2 * y - 1, 16 - 2 * y))
    partner = {
        "sib": {"pool": p + 1 - 2 * c},
        "xp": {"pool": x1 * 4 + zl * 2 + c},
        "xm": {"pool": x3 * 4 + zl * 2 + c},
        "zp": {"pool": p + 2 - 4 * zl},
        **{f"y{e}": {"tp": ALONG_TP[e]} for e in range(8)},
        **{f"r{e}": {"req": e} for e in range(4)},
    }

    main = (main_0, main_1, main_2, main_3)
    over = (over_0, over_1, over_2, over_3)
    cont = (cont_0, cont_1, cont_2, cont_3)

    def device_of(k, i, j):
        return (x + k) % 4 * 4 + (zl + j - 2 * zl * j) * 2 + c + i - 2 * c * i

    locals_ = {}
    for i, (name, src, dst) in enumerate((
        ("table", table_in, table),
        ("suffix", suffix.at[0], cont_0.at[0, 0]),
        ("pool", pool, pool_v),
        ("adapters", adapters_in, adapters),
        ("hidden", hidden.at[0], hid_v),
        ("down", down, down_v),
        ("base", base.at[0], base_v),
        ("up", up, up_v),
        ("plens", plens_in, plens),
        ("slens", slens_in, slens),
        ("wslots", wslots_in, wslots),
    )):
        locals_[name] = pltpu.make_async_copy(src, dst, local_sem.at[i])
        locals_[name].start()

    barrier = pltpu.get_barrier_semaphore()

    def signal(sem, to):
        pl.semaphore_signal(sem, inc=1, device_id=partner[to], device_id_type=MESH)

    for name in NEAR:
        signal(barrier, name)
    for e in range(1, 8):
        pl.when(e > q)(functools.partial(signal, barrier, f"y{e}"))
    for e in range(1, 4):
        pl.when(e > r)(functools.partial(signal, barrier, f"r{e}"))
    pl.semaphore_wait(barrier, len(NEAR) + q + r)
    for e in range(7):
        pl.when(e < q)(functools.partial(signal, here_tp.at[q], f"y{e}"))
    for e in range(3):
        pl.when(e < r)(functools.partial(signal, here_req.at[r], f"r{e}"))

    copies = {}

    def send_to(name, src, dst, to):
        i = len(copies)
        copy = pltpu.make_async_remote_copy(
            src_ref=src, dst_ref=dst,
            send_sem=send_sem.at[i], recv_sem=recv_sem.at[i],
            device_id=partner[to], device_id_type=MESH,
        )
        copies[name] = copy
        copy.start()

    def spread(mine, src, place, sems, names):
        there = [
            pltpu.make_async_remote_copy(
                src_ref=src, dst_ref=place.at[mine],
                send_sem=sems[0].at[e], recv_sem=sems[1].at[mine],
                device_id=partner[name], device_id_type=MESH,
            )
            for e, name in enumerate(names)
        ]
        here = [
            pltpu.make_async_remote_copy(
                src_ref=src, dst_ref=place.at[e],
                send_sem=sems[0].at[e], recv_sem=sems[1].at[e],
                device_id=partner[name], device_id_type=MESH,
            )
            for e, name in enumerate(names)
        ]

        def each(what, copies_):
            for e in range(len(names)):
                pl.when(e != mine)(getattr(copies_[e], what))

        return functools.partial(each, "start", there), functools.partial(each, "wait_recv", here), functools.partial(each, "wait_send", there)

    def send(name, buf, k, at, to):
        there = (k + {"xp": 3, "xm": 1}.get(to, 0)) % 4
        place = list(at)
        if to == "sib":
            place[0] = 1 - at[0]
        if to == "zp":
            place[1] = 1 - at[1]
        send_to(name, buf[k].at[at], buf[there].at[tuple(place)], to)

    def got(*names):
        for name in names:
            copies[name].wait_recv()

    locals_["suffix"].wait()
    send("c_z", cont, 0, (0, 0), "zp")

    def own_slots(tenant):
        def step(b, carry):
            count, picks = carry
            local = table[tenant, b] - p * 20
            owned = (local >= 0) & (local < 20)
            picks = tuple(
                jnp.where(owned & (count == k), local, pick) for k, pick in enumerate(picks)
            )
            return count + owned.astype(jnp.int32), picks

        zero = jnp.int32(0)
        return lax.fori_loop(0, 32, step, (zero, (zero,) * 4), unroll=4)[1]

    locals_["table"].wait()
    mine = own_slots(r)
    locals_["pool"].wait()
    for k in range(2):
        main_0[0, 0, k] = pool_v[mine[k]]
    send("m_p", main, 0, (0, 0), "xp")
    send("m_m", main, 0, (0, 0), "xm")
    send("m_z", main, 0, (0, 0), "zp")

    locals_["hidden"].wait()
    locals_["down"].wait()
    locals_["adapters"].wait()
    adapter = adapters[r]
    part = lax.dot_general(
        down_v[adapter], hid_v[...], (((1,), (1,)), ((), ())), preferred_element_type=jnp.float32
    )
    rank_out[...] = part
    for k in range(2):
        over_0[0, 0, k] = pool_v[mine[2 + k]]
    send("o_z", over, 0, (0, 0), "zp")
    send("m_s", main, 0, (0, 0), "sib")
    for e in range(1, 8):
        pl.when(e > q)(functools.partial(pl.semaphore_wait, here_tp.at[e], 1))
    rank_send, rank_got, rank_sent = spread(
        q, rank_out, rank_in, (rank_ssem, rank_rsem), [f"y{e}" for e in range(8)]
    )
    rank_send()

    got("c_z")
    send("c_p", cont, 0, (0,), "xp")
    send("c_m", cont, 0, (0,), "xm")
    send("c_s", cont, 0, (0,), "sib")

    locals_["plens"].wait()
    plen = plens[r]

    def one_device(d, unused):
        def step(b, carry):
            count, rows = carry
            local = table[r, b] - d * 20
            owned = (local >= 0) & (local < 20)
            seen = plen - b * 128
            rows = tuple(
                jnp.where(owned & (count == k), seen, row) for k, row in enumerate(rows)
            )
            return count + owned.astype(jnp.int32), rows

        zero = jnp.int32(0)
        rows = lax.fori_loop(0, 32, step, (zero, (zero,) * 4), unroll=4)[1]
        for k in range(4):
            nval[d * 4 + k] = rows[k]
        return unused

    lax.fori_loop(0, 16, one_device, 0)

    got("o_z")
    send("o_p", over, 0, (0,), "xp")
    send("o_m", over, 0, (0,), "xm")
    send("o_s", over, 0, (0,), "sib")
    got("m_p")
    send("m_pp", main, 3, (0, 0, 0), "xp")
    send("m_pz", main, 3, (0, 0), "zp")
    send("m_ps", main, 3, (0, 0), "sib")
    got("m_m")
    send("m_mm", main, 1, (0, 0, 1), "xm")
    send("m_mz", main, 1, (0, 0), "zp")
    send("m_ms", main, 1, (0, 0), "sib")
    rank_got()
    total = jnp.zeros(rank_out.shape, jnp.float32)
    for e in range(8):
        total = total + jnp.where(e == q, part, rank_in[e])
    rank = total.T.astype(jnp.bfloat16)
    locals_["base"].wait()
    locals_["up"].wait()
    update = jnp.dot(rank, up_v[adapter], preferred_element_type=jnp.float32)
    query = (base_v[...].astype(jnp.float32) + ADAPTER_SCALING * update).astype(jnp.bfloat16)
    for h in range(8):
        qs[h * 128 : (h + 1) * 128, :] = query[:, h * 128 : (h + 1) * 128]

    peak[...] = jnp.full(peak.shape, LOW, jnp.float32)
    acc[...] = jnp.zeros(acc.shape, jnp.float32)
    scale = HD**-0.5 * LOG2E
    own_key = cont_0[0, 0, 0, 0:1, :]

    row_no = lax.broadcasted_iota(jnp.int32, (128, 128), 0)

    def fill(n, block, rows):
        at = slice(n * 128, (n + 1) * 128)
        seen = row_no < rows
        kc[at, :] = jnp.where(seen, block[0], own_key)
        vc[at, :128] = jnp.where(seen, block[1], jnp.bfloat16(0))
        vc[at, 128:] = jnp.where(seen, jnp.bfloat16(1), jnp.bfloat16(0))

    def attend(size, mask=None):
        keys = kc[:size, :]
        values = vc[:size, :]

        def scores(t):
            rows = slice(t * ROWS, (t + 1) * ROWS)
            s = lax.dot_general(
                qs[rows, :], keys, (((1,), (1,)), ((), ())), preferred_element_type=jnp.float32
            )
            if mask is not None:
                s = jnp.concatenate([s[:, :-512], jnp.where(mask, s[:, -512:], LOW)], axis=1)
            return s

        later = scores(0)
        for t in range(1024 // ROWS):
            rows = slice(t * ROWS, (t + 1) * ROWS)
            s = later
            if t + 1 < 1024 // ROWS:
                later = scores(t + 1)
            old = peak[rows, 0:1]
            new = jnp.maximum(old, jnp.max(s, axis=1, keepdims=True))
            w = jnp.exp2((s - new) * scale).astype(jnp.bfloat16)
            factor = jnp.exp2((old - new) * scale)
            acc[rows, :] = acc[rows, :] * factor + jnp.dot(
                w, values, preferred_element_type=jnp.float32
            )
            peak[rows, :] = jnp.broadcast_to(new, (ROWS, 128))

    def slots(buf, k, first):
        for n in range(8):
            i, j, slot = n // 4, n // 2 % 2, n % 2
            fill(n, buf[k][i, j, slot], nval[device_of(k, i, j) * 4 + first + slot])

    def plane(k):
        slots(main, k, 0)
        for n in range(4):
            fill(8 + n, cont[k][n // 2, n % 2], 128 if k == 0 else jnp.where(x + k >= 4, 128, 0))
        mask = None
        if k == 0:
            lane = lax.broadcasted_iota(jnp.int32, (ROWS, 128), 1)
            token = lax.broadcasted_iota(jnp.int32, (ROWS, 128), 0) + p * 128
            mask = jnp.concatenate(
                [lane + device_of(0, n // 2, n % 2) * 128 <= token for n in range(4)], axis=1
            )
        attend(1536, mask)

    def over_plane(k):
        slots(over, k, 2)
        attend(1024)

    got("m_z", "m_s")
    send("m_zs", main, 0, (0, 1), "sib")
    got("c_s", "m_zs")
    plane(0)

    got("c_p")
    send("c_pp", cont, 3, (0, 0), "xp")
    send("c_ps", cont, 3, (0,), "sib")
    got("c_m")
    send("c_mm", cont, 1, (0, 1), "xm")
    send("c_ms", cont, 1, (0,), "sib")
    got("m_pz", "m_mz")
    send("m_pzs", main, 3, (0, 1), "sib")
    send("m_mzs", main, 1, (0, 1), "sib")
    got("m_pp")
    send("m_ppz", main, 2, (0, 0, 0), "zp")
    send("m_pps", main, 2, (0, 0, 0), "sib")
    got("m_mm")
    send("m_mmz", main, 2, (0, 0, 1), "zp")
    send("m_mms", main, 2, (0, 0, 1), "sib")
    got("m_ps", "m_pzs", "c_ps")
    plane(3)

    got("c_pp")
    send("c_pps", cont, 2, (0, 0), "sib")
    got("c_mm")
    send("c_mms", cont, 2, (0, 1), "sib")
    got("m_ppz", "m_mmz")
    send("m_zzs", main, 2, (0, 1), "sib")
    got("m_ms", "m_mzs", "c_ms")
    plane(1)

    got("o_p")
    send("o_pp", over, 3, (0, 0), "xp")
    send("o_ps", over, 3, (0,), "sib")
    got("o_m")
    send("o_mm", over, 1, (0, 1), "xm")
    send("o_ms", over, 1, (0,), "sib")
    got("c_pps", "c_mms")

    locals_["wslots"].wait()

    def write_step(b, block):
        local = wslots[r, b] - p * 20
        return jnp.where((local >= 0) & (local < 20), b, block)

    block = lax.fori_loop(0, 16, write_step, jnp.int32(0), unroll=4)
    i, j = (block + c) % 2, (block // 2 + zl) % 2
    away = (block // 4 + 4 - x) % 4
    chosen = cont_0[i, j]
    for k in range(1, 4):
        chosen = jnp.where(away == k, cont[k][i, j], chosen)
    wmine[...] = chosen
    for e in range(1, 4):
        pl.when(e > r)(functools.partial(pl.semaphore_wait, here_req.at[e], 1))
    write_send, write_got, write_sent = spread(
        r, wmine, wblk, (write_ssem, write_rsem), [f"r{e}" for e in range(4)]
    )
    write_send()

    got("m_pps", "m_mms", "m_zzs")
    plane(2)
    got("o_pp")
    send("o_pps", over, 2, (0, 0), "sib")
    got("o_mm")
    send("o_mms", over, 2, (0, 1), "sib")
    got("o_s")
    over_plane(0)
    got("o_ps")
    over_plane(3)
    got("o_ms")
    over_plane(1)
    got("o_pps", "o_mms")
    over_plane(2)

    write_got()
    for e in range(4):
        writes[e] = jnp.where(e == r, wmine[...], wblk[e])

    token = p * 128 + lax.broadcasted_iota(jnp.int32, (128, 128), 0)
    locals_["slens"].wait()
    live = token < slens[r]
    for h in range(8):
        rows = slice(h * 128, (h + 1) * 128)
        value = acc[rows, :128] / acc[rows, 128:]
        out[0, :, rows] = jnp.where(live, value, 0.0).astype(jnp.bfloat16)

    for copy in copies.values():
        copy.wait_send()
    rank_sent()
    write_sent()


def place(wslots, attended_in, writes, pool, attended, pool_after, sems):
    p = lax.axis_index("pool")
    hand_on = pltpu.make_async_copy(attended_in, attended, sems.at[20])
    hand_on.start()

    def find(tenant):
        def step(b, slot):
            local = wslots[tenant, b] - p * 20
            return jnp.where((local >= 0) & (local < 20), local, slot)

        return lax.fori_loop(0, 16, step, jnp.int32(0), unroll=4)

    slots = [find(tenant) for tenant in range(4)]
    for s in range(20):
        kept = True
        for tenant, slot in enumerate(slots):
            kept = kept & (slot != s)
            pl.when(slot == s)(
                pltpu.make_async_copy(writes.at[tenant], pool_after.at[s], sems.at[s]).start
            )
        pl.when(kept)(pltpu.make_async_copy(pool.at[s], pool_after.at[s], sems.at[s]).start)
    for s in range(20):
        pltpu.make_async_copy(pool.at[s], pool_after.at[s], sems.at[s]).wait()
    hand_on.wait()


def local(hidden, base, suffix, pool, down, up, table, plens, slens, adapters, wslots):
    bf, f32 = jnp.bfloat16, jnp.float32
    down = down.transpose(0, 2, 1)
    hbm = pl.BlockSpec(memory_space=pltpu.HBM)
    vmem = pl.BlockSpec(memory_space=pltpu.VMEM)
    block = (2, 128, 128)
    attended, writes = pl.pallas_call(
        kernel,
        out_shape=(
            jax.ShapeDtypeStruct(base.shape, bf),
            jax.ShapeDtypeStruct((4,) + block, bf),
        ),
        in_specs=[hbm] * 11,
        out_specs=(vmem, vmem),
        scratch_shapes=[
            *[pltpu.SMEM(a.shape, jnp.int32) for a in (table, plens, slens, adapters, wslots)],
            pltpu.VMEM(pool.shape, bf),
            pltpu.VMEM(hidden.shape[1:], bf),
            pltpu.VMEM(base.shape[1:], bf),
            pltpu.VMEM(down.shape, bf),
            pltpu.VMEM(up.shape, bf),
            *[pltpu.VMEM((2, 2, 2) + block, bf)] * 8,
            *[pltpu.VMEM((2, 2) + block, bf)] * 4,
            pltpu.VMEM((4,) + block, bf),
            pltpu.VMEM(block, bf),
            pltpu.VMEM((16, 128), f32),
            pltpu.VMEM((8, 16, 128), f32),
            pltpu.VMEM((1024, 128), bf),
            pltpu.VMEM((1024, 128), f32),
            pltpu.VMEM((1024, 256), f32),
            pltpu.VMEM((1536, 128), bf),
            pltpu.VMEM((1536, 256), bf),
            pltpu.SMEM((64,), jnp.int32),
            pltpu.SemaphoreType.DMA((11,)),
            pltpu.SemaphoreType.DMA((COPIES,)),
            pltpu.SemaphoreType.DMA((COPIES,)),
            pltpu.SemaphoreType.DMA((8,)),
            pltpu.SemaphoreType.DMA((8,)),
            pltpu.SemaphoreType.DMA((4,)),
            pltpu.SemaphoreType.DMA((4,)),
            pltpu.SemaphoreType.REGULAR((8,)),
            pltpu.SemaphoreType.REGULAR((4,)),
        ],
        compiler_params=pltpu.CompilerParams(
            collective_id=0, has_side_effects=True, vmem_limit_bytes=62 << 20
        ),
        name="attend_all",
    )(table, plens, slens, adapters, wslots, hidden, base, suffix, pool, down, up)
    return pl.pallas_call(
        place,
        out_shape=(
            jax.ShapeDtypeStruct(base.shape, bf),
            jax.ShapeDtypeStruct(pool.shape, bf),
        ),
        in_specs=[pl.BlockSpec(memory_space=pltpu.SMEM)] + [hbm] * 3,
        out_specs=(hbm, hbm),
        scratch_shapes=[pltpu.SemaphoreType.DMA((21,))],
        compiler_params=pltpu.CompilerParams(vmem_limit_bytes=62 << 20),
        name="place",
    )(wslots, attended, writes, pool)


def solution(mesh):
    in_specs = (
        P("req", "pool", "tp"),
        P("req", "pool", "tp"),
        P("req", None, "pool", "tp"),
        P("pool", None, None, "tp"),
        P(None, "tp", None),
        P(None, None, "tp"),
        P(),
        P(),
        P(),
        P(),
        P(),
    )
    out_specs = (P("req", "pool", "tp"), P("pool", None, None, "tp"))
    return jax.shard_map(local, mesh=mesh, in_specs=in_specs, out_specs=out_specs, check_vma=False)
```

```python
import functools

import jax
import jax.numpy as jnp
from jax import lax
from jax.experimental import pallas as pl
from jax.experimental.pallas import tpu as pltpu
from jax.sharding import PartitionSpec as P

MESH = pl.DeviceIdType.MESH
HD = 128
ADAPTER_SCALING = 0.5
LOG2E = 1.4426950408889634
LOW = -1e30
ROWS = 128
NEAR = ("sib", "xp", "xm", "zp")
ALONG_TP = (0, 1, 7, 2, 6, 3, 5, 4)
COPIES = 38


def kernel(
    table_in, plens_in, slens_in, adapters_in, wslots_in,
    hidden, base, suffix, pool, down, up,
    out, writes,
    table, plens, slens, adapters, wslots,
    pool_v, hid_v, base_v, down_v, up_v,
    main_0, main_1, main_2, main_3, over_0, over_1, over_2, over_3, cont_0, cont_1, cont_2, cont_3,
    wblk, wmine,
    rank_out, rank_in, qs, peak, acc, kc, vc, lines, nval,
    local_sem, send_sem, recv_sem, rank_ssem, rank_rsem, write_ssem, write_rsem, here_tp, here_req,
):
    p = lax.axis_index("pool")
    y = lax.axis_index("tp")
    r = lax.axis_index("req")
    x, zl, c = p // 4, (p // 2) % 2, p % 2
    x1, x3 = (x + 1) % 4, (x + 3) % 4
    q = jnp.where(y == 0, 0, jnp.where(y <= 4, 2 * y - 1, 16 - 2 * y))
    partner = {
        "sib": {"pool": p + 1 - 2 * c},
        "xp": {"pool": x1 * 4 + zl * 2 + c},
        "xm": {"pool": x3 * 4 + zl * 2 + c},
        "zp": {"pool": p + 2 - 4 * zl},
        **{f"y{e}": {"tp": ALONG_TP[e]} for e in range(8)},
        **{f"r{e}": {"req": e} for e in range(4)},
    }

    main = (main_0, main_1, main_2, main_3)
    over = (over_0, over_1, over_2, over_3)
    cont = (cont_0, cont_1, cont_2, cont_3)

    def device_of(k, i, j):
        return (x + k) % 4 * 4 + (zl + j - 2 * zl * j) * 2 + c + i - 2 * c * i

    locals_ = {}
    for i, (name, src, dst) in enumerate((
        ("table", table_in, table),
        ("suffix", suffix.at[0], cont_0.at[0, 0]),
        ("pool", pool, pool_v),
        ("adapters", adapters_in, adapters),
        ("hidden", hidden.at[0], hid_v),
        ("down", down, down_v),
        ("base", base.at[0], base_v),
        ("up", up, up_v),
        ("plens", plens_in, plens),
        ("lines", table_in, lines),
        ("slens", slens_in, slens),
        ("wslots", wslots_in, wslots),
    )):
        locals_[name] = pltpu.make_async_copy(src, dst, local_sem.at[i])
        locals_[name].start()

    barrier = pltpu.get_barrier_semaphore()

    def signal(sem, to):
        pl.semaphore_signal(sem, inc=1, device_id=partner[to], device_id_type=MESH)

    for name in NEAR:
        signal(barrier, name)
    for e in range(1, 8):
        pl.when(e > q)(functools.partial(signal, barrier, f"y{e}"))
    for e in range(1, 4):
        pl.when(e > r)(functools.partial(signal, barrier, f"r{e}"))
    pl.semaphore_wait(barrier, len(NEAR) + q + r)
    for e in range(7):
        pl.when(e < q)(functools.partial(signal, here_tp.at[q], f"y{e}"))
    for e in range(3):
        pl.when(e < r)(functools.partial(signal, here_req.at[r], f"r{e}"))

    copies = {}

    def send_to(name, src, dst, to):
        i = len(copies)
        copy = pltpu.make_async_remote_copy(
            src_ref=src, dst_ref=dst,
            send_sem=send_sem.at[i], recv_sem=recv_sem.at[i],
            device_id=partner[to], device_id_type=MESH,
        )
        copies[name] = copy
        copy.start()

    def spread(mine, src, place, sems, names):
        there = [
            pltpu.make_async_remote_copy(
                src_ref=src, dst_ref=place.at[mine],
                send_sem=sems[0].at[e], recv_sem=sems[1].at[mine],
                device_id=partner[name], device_id_type=MESH,
            )
            for e, name in enumerate(names)
        ]
        here = [
            pltpu.make_async_remote_copy(
                src_ref=src, dst_ref=place.at[e],
                send_sem=sems[0].at[e], recv_sem=sems[1].at[e],
                device_id=partner[name], device_id_type=MESH,
            )
            for e, name in enumerate(names)
        ]

        def each(what, copies_):
            for e in range(len(names)):
                pl.when(e != mine)(getattr(copies_[e], what))

        return functools.partial(each, "start", there), functools.partial(each, "wait_recv", here), functools.partial(each, "wait_send", there)

    def send(name, buf, k, at, to):
        there = (k + {"xp": 3, "xm": 1}.get(to, 0)) % 4
        place = list(at)
        if to == "sib":
            place[0] = 1 - at[0]
        if to == "zp":
            place[1] = 1 - at[1]
        send_to(name, buf[k].at[at], buf[there].at[tuple(place)], to)

    def got(*names):
        for name in names:
            copies[name].wait_recv()

    locals_["suffix"].wait()
    send("c_z", cont, 0, (0, 0), "zp")

    def own_slots(tenant):
        def step(b, carry):
            count, picks = carry
            local = table[tenant, b] - p * 20
            owned = (local >= 0) & (local < 20)
            picks = tuple(
                jnp.where(owned & (count == k), local, pick) for k, pick in enumerate(picks)
            )
            return count + owned.astype(jnp.int32), picks

        zero = jnp.int32(0)
        return lax.fori_loop(0, 32, step, (zero, (zero,) * 4), unroll=4)[1]

    locals_["table"].wait()
    mine = own_slots(r)
    locals_["pool"].wait()
    for k in range(2):
        main_0[0, 0, k] = pool_v[mine[k]]
    send("m_p", main, 0, (0, 0), "xp")
    send("m_m", main, 0, (0, 0), "xm")
    for k in range(2):
        over_0[0, 0, k] = pool_v[mine[2 + k]]
    send("o_z", over, 0, (0, 0), "zp")

    locals_["hidden"].wait()
    locals_["down"].wait()
    locals_["adapters"].wait()
    adapter = adapters[r]
    part = lax.dot_general(
        down_v[adapter], hid_v[...], (((1,), (1,)), ((), ())), preferred_element_type=jnp.float32
    )
    rank_out[...] = part

    got("c_z")
    send("c_p", cont, 0, (0,), "xp")
    send("c_m", cont, 0, (0,), "xm")
    send("c_s", cont, 0, (0,), "sib")
    send("m_z", main, 0, (0, 0), "zp")
    send("m_s", main, 0, (0, 0), "sib")
    for e in range(1, 8):
        pl.when(e > q)(functools.partial(pl.semaphore_wait, here_tp.at[e], 1))
    rank_send, rank_got, rank_sent = spread(
        q, rank_out, rank_in, (rank_ssem, rank_rsem), [f"y{e}" for e in range(8)]
    )
    rank_send()

    locals_["plens"].wait()
    locals_["lines"].wait()
    device = lax.broadcasted_iota(jnp.int32, (16, 32), 0) * 20
    line = lines[pl.ds(r, 1), :]
    owned = ((line >= device) & (line < device + 20)).astype(jnp.float32)
    before = lax.broadcasted_iota(jnp.int32, (32, 32), 0) < lax.broadcasted_iota(jnp.int32, (32, 32), 1)
    order = jnp.dot(
        owned.astype(jnp.bfloat16), before.astype(jnp.bfloat16), preferred_element_type=jnp.float32
    )
    rest = (plens[r] - lax.broadcasted_iota(jnp.int32, (16, 32), 1) * 128).astype(jnp.float32)
    for k in range(4):
        rows = jnp.sum(jnp.where(order == k, owned * rest, 0.0), axis=1, keepdims=True)
        nval[k] = jnp.broadcast_to(rows, (16, 128))

    got("m_p")
    send("m_pp", main, 3, (0, 0, 0), "xp")
    send("m_pz", main, 3, (0, 0), "zp")
    send("m_ps", main, 3, (0, 0), "sib")
    got("m_m")
    send("m_mm", main, 1, (0, 0, 1), "xm")
    send("m_mz", main, 1, (0, 0), "zp")
    send("m_ms", main, 1, (0, 0), "sib")
    rank_got()
    total = jnp.zeros(rank_out.shape, jnp.float32)
    for e in range(8):
        total = total + jnp.where(e == q, part, rank_in[e])
    rank = total.T.astype(jnp.bfloat16)
    locals_["base"].wait()
    locals_["up"].wait()
    update = jnp.dot(rank, up_v[adapter], preferred_element_type=jnp.float32)
    query = (base_v[...].astype(jnp.float32) + ADAPTER_SCALING * update).astype(jnp.bfloat16)
    for h in range(8):
        qs[h * 128 : (h + 1) * 128, :] = query[:, h * 128 : (h + 1) * 128]

    peak[...] = jnp.full(peak.shape, LOW, jnp.float32)
    acc[...] = jnp.zeros(acc.shape, jnp.float32)
    scale = HD**-0.5 * LOG2E
    own_key = cont_0[0, 0, 0, 0:1, :]

    row_no = lax.broadcasted_iota(jnp.int32, (128, 128), 0).astype(jnp.float32)

    def fill(n, block, rows):
        at = slice(n * 128, (n + 1) * 128)
        seen = row_no < rows
        kc[at, :] = jnp.where(seen, block[0], own_key)
        vc[at, :128] = jnp.where(seen, block[1], jnp.bfloat16(0))
        vc[at, 128:] = jnp.where(seen, jnp.bfloat16(1), jnp.bfloat16(0))

    def attend(size, mask=None):
        keys = kc[:size, :]
        values = vc[:size, :]

        def scores(t):
            rows = slice(t * ROWS, (t + 1) * ROWS)
            s = lax.dot_general(
                qs[rows, :], keys, (((1,), (1,)), ((), ())), preferred_element_type=jnp.float32
            )
            if mask is not None:
                s = jnp.concatenate([s[:, :-512], jnp.where(mask, s[:, -512:], LOW)], axis=1)
            return s

        later = scores(0)
        for t in range(1024 // ROWS):
            rows = slice(t * ROWS, (t + 1) * ROWS)
            s = later
            if t + 1 < 1024 // ROWS:
                later = scores(t + 1)
            old = peak[rows, 0:1]
            new = jnp.maximum(old, jnp.max(s, axis=1, keepdims=True))
            w = jnp.exp2((s - new) * scale).astype(jnp.bfloat16)
            factor = jnp.exp2((old - new) * scale)
            acc[rows, :] = acc[rows, :] * factor + jnp.dot(
                w, values, preferred_element_type=jnp.float32
            )
            peak[rows, :] = jnp.broadcast_to(new, (ROWS, 128))

    def slots(buf, k, first):
        for n in range(8):
            i, j, slot = n // 4, n // 2 % 2, n % 2
            fill(n, buf[k][i, j, slot], nval[first + slot, pl.ds(device_of(k, i, j), 1), :])

    def plane(k):
        slots(main, k, 0)
        for n in range(4):
            fill(8 + n, cont[k][n // 2, n % 2], 128.0 if k == 0 else jnp.where(x + k >= 4, 128.0, 0.0))
        mask = None
        if k == 0:
            lane = lax.broadcasted_iota(jnp.int32, (ROWS, 128), 1)
            token = lax.broadcasted_iota(jnp.int32, (ROWS, 128), 0) + p * 128
            mask = jnp.concatenate(
                [lane + device_of(0, n // 2, n % 2) * 128 <= token for n in range(4)], axis=1
            )
        attend(1536, mask)

    def over_plane(k):
        slots(over, k, 2)
        attend(1024)

    got("c_p")
    send("c_pp", cont, 3, (0, 0), "xp")
    send("c_ps", cont, 3, (0,), "sib")
    got("c_m")
    send("c_mm", cont, 1, (0, 1), "xm")
    send("c_ms", cont, 1, (0,), "sib")
    got("o_z")
    send("o_p", over, 0, (0,), "xp")
    send("o_m", over, 0, (0,), "xm")
    send("o_s", over, 0, (0,), "sib")

    got("m_z", "m_s")
    send("m_zs", main, 0, (0, 1), "sib")
    got("c_s", "m_zs")
    plane(0)

    got("c_pp")
    send("c_pps", cont, 2, (0, 0), "sib")
    got("c_mm")
    send("c_mms", cont, 2, (0, 1), "sib")
    got("m_pz", "m_mz")
    send("m_pzs", main, 3, (0, 1), "sib")
    send("m_mzs", main, 1, (0, 1), "sib")
    got("m_pp")
    send("m_ppz", main, 2, (0, 0, 0), "zp")
    send("m_pps", main, 2, (0, 0, 0), "sib")
    got("m_mm")
    send("m_mmz", main, 2, (0, 0, 1), "zp")
    send("m_mms", main, 2, (0, 0, 1), "sib")
    got("m_ps", "m_pzs", "c_ps")
    plane(3)

    got("c_ms", "c_pps", "c_mms")

    locals_["wslots"].wait()

    def write_step(b, block):
        local = wslots[r, b] - p * 20
        return jnp.where((local >= 0) & (local < 20), b, block)

    block = lax.fori_loop(0, 16, write_step, jnp.int32(0), unroll=4)
    i, j = (block + c) % 2, (block // 2 + zl) % 2
    away = (block // 4 + 4 - x) % 4
    chosen = cont_0[i, j]
    for k in range(1, 4):
        chosen = jnp.where(away == k, cont[k][i, j], chosen)
    wmine[...] = chosen
    for e in range(1, 4):
        pl.when(e > r)(functools.partial(pl.semaphore_wait, here_req.at[e], 1))
    write_send, write_got, write_sent = spread(
        r, wmine, wblk, (write_ssem, write_rsem), [f"r{e}" for e in range(4)]
    )
    write_send()

    got("o_p")
    send("o_pp", over, 3, (0, 0), "xp")
    send("o_ps", over, 3, (0,), "sib")
    got("o_m")
    send("o_mm", over, 1, (0, 1), "xm")
    send("o_ms", over, 1, (0,), "sib")
    got("m_ppz", "m_mmz")
    send("m_zzs", main, 2, (0, 1), "sib")
    got("m_ms", "m_mzs")
    plane(1)

    got("m_pps", "m_mms", "m_zzs")
    plane(2)
    got("o_pp")
    send("o_pps", over, 2, (0, 0), "sib")
    got("o_mm")
    send("o_mms", over, 2, (0, 1), "sib")
    got("o_s")
    over_plane(0)
    got("o_ps")
    over_plane(3)
    got("o_ms")
    over_plane(1)
    got("o_pps", "o_mms")
    over_plane(2)

    write_got()
    for e in range(4):
        writes[e] = jnp.where(e == r, wmine[...], wblk[e])

    token = p * 128 + lax.broadcasted_iota(jnp.int32, (128, 128), 0)
    locals_["slens"].wait()
    live = token < slens[r]
    for h in range(8):
        rows = slice(h * 128, (h + 1) * 128)
        value = acc[rows, :128] / acc[rows, 128:]
        out[0, :, rows] = jnp.where(live, value, 0.0).astype(jnp.bfloat16)

    for copy in copies.values():
        copy.wait_send()
    rank_sent()
    write_sent()


def place(wslots, attended_in, writes, pool, attended, pool_after, held, blocks, in_sem, out_sem):
    p = lax.axis_index("pool")
    first = pltpu.make_async_copy(attended_in, held, in_sem.at[20])
    second = pltpu.make_async_copy(held, attended, out_sem.at[20])
    first.start()

    def find(tenant):
        def step(b, slot):
            local = wslots[tenant, b] - p * 20
            return jnp.where((local >= 0) & (local < 20), local, slot)

        return lax.fori_loop(0, 16, step, jnp.int32(0), unroll=4)

    slots = [find(tenant) for tenant in range(4)]
    for s in range(20):
        kept = True
        for tenant, slot in enumerate(slots):
            kept = kept & (slot != s)
            pl.when(slot == s)(
                pltpu.make_async_copy(writes.at[tenant], blocks.at[s], in_sem.at[s]).start
            )
        pl.when(kept)(pltpu.make_async_copy(pool.at[s], blocks.at[s], in_sem.at[s]).start)
    first.wait()
    second.start()
    for s in range(20):
        pltpu.make_async_copy(pool.at[s], blocks.at[s], in_sem.at[s]).wait()
        pltpu.make_async_copy(blocks.at[s], pool_after.at[s], out_sem.at[s]).start()
    for s in range(20):
        pltpu.make_async_copy(blocks.at[s], pool_after.at[s], out_sem.at[s]).wait()
    second.wait()


def local(hidden, base, suffix, pool, down, up, table, plens, slens, adapters, wslots):
    bf, f32 = jnp.bfloat16, jnp.float32
    down = down.transpose(0, 2, 1)
    hbm = pl.BlockSpec(memory_space=pltpu.HBM)
    vmem = pl.BlockSpec(memory_space=pltpu.VMEM)
    block = (2, 128, 128)
    attended, writes = pl.pallas_call(
        kernel,
        out_shape=(
            jax.ShapeDtypeStruct(base.shape, bf),
            jax.ShapeDtypeStruct((4,) + block, bf),
        ),
        in_specs=[hbm] * 11,
        out_specs=(vmem, vmem),
        scratch_shapes=[
            *[pltpu.SMEM(a.shape, jnp.int32) for a in (table, plens, slens, adapters, wslots)],
            pltpu.VMEM(pool.shape, bf),
            pltpu.VMEM(hidden.shape[1:], bf),
            pltpu.VMEM(base.shape[1:], bf),
            pltpu.VMEM(down.shape, bf),
            pltpu.VMEM(up.shape, bf),
            *[pltpu.VMEM((2, 2, 2) + block, bf)] * 8,
            *[pltpu.VMEM((2, 2) + block, bf)] * 4,
            pltpu.VMEM((4,) + block, bf),
            pltpu.VMEM(block, bf),
            pltpu.VMEM((16, 128), f32),
            pltpu.VMEM((8, 16, 128), f32),
            pltpu.VMEM((1024, 128), bf),
            pltpu.VMEM((1024, 128), f32),
            pltpu.VMEM((1024, 256), f32),
            pltpu.VMEM((1536, 128), bf),
            pltpu.VMEM((1536, 256), bf),
            pltpu.VMEM(table.shape, jnp.int32),
            pltpu.VMEM((4, 16, 128), f32),
            pltpu.SemaphoreType.DMA((12,)),
            pltpu.SemaphoreType.DMA((COPIES,)),
            pltpu.SemaphoreType.DMA((COPIES,)),
            pltpu.SemaphoreType.DMA((8,)),
            pltpu.SemaphoreType.DMA((8,)),
            pltpu.SemaphoreType.DMA((4,)),
            pltpu.SemaphoreType.DMA((4,)),
            pltpu.SemaphoreType.REGULAR((8,)),
            pltpu.SemaphoreType.REGULAR((4,)),
        ],
        compiler_params=pltpu.CompilerParams(
            collective_id=0, has_side_effects=True, vmem_limit_bytes=62 << 20
        ),
        name="attend_all",
    )(table, plens, slens, adapters, wslots, hidden, base, suffix, pool, down, up)
    return pl.pallas_call(
        place,
        out_shape=(
            jax.ShapeDtypeStruct(base.shape, bf),
            jax.ShapeDtypeStruct(pool.shape, bf),
        ),
        in_specs=[pl.BlockSpec(memory_space=pltpu.SMEM)] + [hbm] * 3,
        out_specs=(hbm, hbm),
        scratch_shapes=[
            pltpu.VMEM(base.shape, bf),
            pltpu.VMEM(pool.shape, bf),
            pltpu.SemaphoreType.DMA((21,)),
            pltpu.SemaphoreType.DMA((21,)),
        ],
        compiler_params=pltpu.CompilerParams(vmem_limit_bytes=62 << 20),
        name="place",
    )(wslots, attended, writes, pool)


def solution(mesh):
    in_specs = (
        P("req", "pool", "tp"),
        P("req", "pool", "tp"),
        P("req", None, "pool", "tp"),
        P("pool", None, None, "tp"),
        P(None, "tp", None),
        P(None, None, "tp"),
        P(),
        P(),
        P(),
        P(),
        P(),
    )
    out_specs = (P("req", "pool", "tp"), P("pool", None, None, "tp"))
    return jax.shard_map(local, mesh=mesh, in_specs=in_specs, out_specs=out_specs, check_vma=False)
```

```python
import functools

import jax
import jax.numpy as jnp
from jax import lax
from jax.experimental import pallas as pl
from jax.experimental.pallas import tpu as pltpu
from jax.sharding import PartitionSpec as P

MESH = pl.DeviceIdType.MESH
HD = 128
ADAPTER_SCALING = 0.5
LOG2E = 1.4426950408889634
LOW = -1e30
ROWS = 128
NEAR = ("sib", "xp", "xm", "zp")
ALONG_TP = (0, 1, 7, 2, 6, 3, 5, 4)
COPIES = 38


def kernel(
    table_in, plens_in, slens_in, adapters_in, wslots_in,
    hidden, base, suffix, pool, down, up,
    out, writes,
    table, plens, slens, adapters, wslots,
    pool_v, hid_v, base_v, down_v, up_v,
    main_0, main_1, main_2, main_3, over_all, cont_0, cont_1, cont_2, cont_3,
    wblk, wmine,
    rank_out, rank_in, qs, peak, acc, kc, vc, lines, nval, list_v, listed,
    local_sem, send_sem, recv_sem, rank_ssem, rank_rsem, write_ssem, write_rsem, here_tp, here_req,
):
    p = lax.axis_index("pool")
    y = lax.axis_index("tp")
    r = lax.axis_index("req")
    x, zl, c = p // 4, (p // 2) % 2, p % 2
    x1, x3 = (x + 1) % 4, (x + 3) % 4
    q = jnp.where(y == 0, 0, jnp.where(y <= 4, 2 * y - 1, 16 - 2 * y))
    partner = {
        "sib": {"pool": p + 1 - 2 * c},
        "xp": {"pool": x1 * 4 + zl * 2 + c},
        "xm": {"pool": x3 * 4 + zl * 2 + c},
        "zp": {"pool": p + 2 - 4 * zl},
        **{f"y{e}": {"tp": ALONG_TP[e]} for e in range(8)},
        **{f"r{e}": {"req": e} for e in range(4)},
    }

    main = (main_0, main_1, main_2, main_3)
    over = [over_all.at[k] for k in range(4)]
    cont = (cont_0, cont_1, cont_2, cont_3)

    def device_of(k, i, j):
        return (x + k) % 4 * 4 + (zl + j - 2 * zl * j) * 2 + c + i - 2 * c * i

    locals_ = {}
    for i, (name, src, dst) in enumerate((
        ("table", table_in, table),
        ("suffix", suffix.at[0], cont_0.at[0, 0]),
        ("pool", pool, pool_v),
        ("adapters", adapters_in, adapters),
        ("hidden", hidden.at[0], hid_v),
        ("down", down, down_v),
        ("base", base.at[0], base_v),
        ("up", up, up_v),
        ("plens", plens_in, plens),
        ("lines", table_in, lines),
        ("slens", slens_in, slens),
        ("wslots", wslots_in, wslots),
    )):
        locals_[name] = pltpu.make_async_copy(src, dst, local_sem.at[i])
        locals_[name].start()

    barrier = pltpu.get_barrier_semaphore()

    def signal(sem, to):
        pl.semaphore_signal(sem, inc=1, device_id=partner[to], device_id_type=MESH)

    for name in NEAR:
        signal(barrier, name)
    for e in range(1, 8):
        pl.when(e > q)(functools.partial(signal, barrier, f"y{e}"))
    for e in range(1, 4):
        pl.when(e > r)(functools.partial(signal, barrier, f"r{e}"))
    pl.semaphore_wait(barrier, len(NEAR) + q + r)
    for e in range(7):
        pl.when(e < q)(functools.partial(signal, here_tp.at[q], f"y{e}"))
    for e in range(3):
        pl.when(e < r)(functools.partial(signal, here_req.at[r], f"r{e}"))

    copies = {}

    def send_to(name, src, dst, to):
        i = len(copies)
        copy = pltpu.make_async_remote_copy(
            src_ref=src, dst_ref=dst,
            send_sem=send_sem.at[i], recv_sem=recv_sem.at[i],
            device_id=partner[to], device_id_type=MESH,
        )
        copies[name] = copy
        copy.start()

    def spread(mine, src, place, sems, names):
        there = [
            pltpu.make_async_remote_copy(
                src_ref=src, dst_ref=place.at[mine],
                send_sem=sems[0].at[e], recv_sem=sems[1].at[mine],
                device_id=partner[name], device_id_type=MESH,
            )
            for e, name in enumerate(names)
        ]
        here = [
            pltpu.make_async_remote_copy(
                src_ref=src, dst_ref=place.at[e],
                send_sem=sems[0].at[e], recv_sem=sems[1].at[e],
                device_id=partner[name], device_id_type=MESH,
            )
            for e, name in enumerate(names)
        ]

        def each(what, copies_):
            for e in range(len(names)):
                pl.when(e != mine)(getattr(copies_[e], what))

        return functools.partial(each, "start", there), functools.partial(each, "wait_recv", here), functools.partial(each, "wait_send", there)

    def send(name, buf, k, at, to):
        there = (k + {"xp": 3, "xm": 1}.get(to, 0)) % 4
        place = list(at)
        if to == "sib":
            place[0] = 1 - at[0]
        if to == "zp":
            place[1] = 1 - at[1]
        send_to(name, buf[k].at[at], buf[there].at[tuple(place)], to)

    def got(*names):
        for name in names:
            copies[name].wait_recv()

    locals_["suffix"].wait()
    send("c_z", cont, 0, (0, 0), "zp")

    def own_slots(tenant):
        def step(b, carry):
            count, picks = carry
            local = table[tenant, b] - p * 20
            owned = (local >= 0) & (local < 20)
            picks = tuple(
                jnp.where(owned & (count == k), local, pick) for k, pick in enumerate(picks)
            )
            return count + owned.astype(jnp.int32), picks

        zero = jnp.int32(0)
        return lax.fori_loop(0, 32, step, (zero, (zero,) * 4), unroll=4)[1]

    locals_["table"].wait()
    mine = own_slots(r)
    locals_["pool"].wait()
    for k in range(2):
        main_0[0, 0, k] = pool_v[mine[k]]
    send("m_p", main, 0, (0, 0), "xp")
    send("m_m", main, 0, (0, 0), "xm")
    for k in range(2):
        over_all[0, 0, 0, k] = pool_v[mine[2 + k]]
    send("o_z", over, 0, (0, 0), "zp")
    send("m_s", main, 0, (0, 0), "sib")

    locals_["hidden"].wait()
    locals_["down"].wait()
    locals_["adapters"].wait()
    adapter = adapters[r]
    part = lax.dot_general(
        down_v[adapter], hid_v[...], (((1,), (1,)), ((), ())), preferred_element_type=jnp.float32
    )
    rank_out[...] = part

    got("c_z")
    send("c_p", cont, 0, (0,), "xp")
    send("c_m", cont, 0, (0,), "xm")
    send("c_s", cont, 0, (0,), "sib")
    send("m_z", main, 0, (0, 0), "zp")
    for e in range(1, 8):
        pl.when(e > q)(functools.partial(pl.semaphore_wait, here_tp.at[e], 1))
    rank_send, rank_got, rank_sent = spread(
        q, rank_out, rank_in, (rank_ssem, rank_rsem), [f"y{e}" for e in range(8)]
    )
    rank_send()

    locals_["plens"].wait()
    locals_["lines"].wait()
    device = lax.broadcasted_iota(jnp.int32, (16, 32), 0) * 20
    line = lines[pl.ds(r, 1), :]
    owned = ((line >= device) & (line < device + 20)).astype(jnp.float32)
    before = lax.broadcasted_iota(jnp.int32, (32, 32), 0) < lax.broadcasted_iota(jnp.int32, (32, 32), 1)
    order = jnp.dot(
        owned.astype(jnp.bfloat16), before.astype(jnp.bfloat16), preferred_element_type=jnp.float32
    )
    rest = (plens[r] - lax.broadcasted_iota(jnp.int32, (16, 32), 1) * 128).astype(jnp.float32)
    for k in range(4):
        rows = jnp.sum(jnp.where(order == k, owned * rest, 0.0), axis=1, keepdims=True)
        nval[k] = jnp.broadcast_to(rows, (16, 128))
    more = jnp.maximum(jnp.sum(owned, axis=1, keepdims=True) - 2.0, 0.0)
    more = jnp.broadcast_to(more, (16, 128))
    above = lax.broadcasted_iota(jnp.int32, (16, 16), 1) < lax.broadcasted_iota(jnp.int32, (16, 16), 0)
    ahead = jnp.dot(
        above.astype(jnp.bfloat16), more.astype(jnp.bfloat16), preferred_element_type=jnp.float32
    )
    lane = lax.broadcasted_iota(jnp.int32, (16, 128), 1).astype(jnp.float32)
    number = lax.broadcasted_iota(jnp.int32, (16, 128), 0).astype(jnp.float32)
    third = jnp.where((more > 0.5) & (ahead == lane), 1.0, 0.0)
    fourth = jnp.where((more > 1.5) & (ahead + 1.0 == lane), 1.0, 0.0)
    names = jnp.sum(third * (2.0 * number) + fourth * (2.0 * number + 1.0), axis=0, keepdims=True)
    rows = jnp.sum(third * nval[2] + fourth * nval[3], axis=0, keepdims=True)
    list_v[...] = jnp.zeros(list_v.shape, jnp.int32)
    list_v[0:1, :] = names.astype(jnp.int32)
    list_v[1:2, :] = rows.astype(jnp.int32)
    list_copy = pltpu.make_async_copy(list_v, listed, local_sem.at[12])
    list_copy.start()

    got("m_p")
    send("m_pp", main, 3, (0, 0, 0), "xp")
    send("m_pz", main, 3, (0, 0), "zp")
    send("m_ps", main, 3, (0, 0), "sib")
    got("m_m")
    send("m_mm", main, 1, (0, 0, 1), "xm")
    send("m_mz", main, 1, (0, 0), "zp")
    send("m_ms", main, 1, (0, 0), "sib")
    got("o_z")
    send("o_p", over, 0, (0,), "xp")
    send("o_m", over, 0, (0,), "xm")
    send("o_s", over, 0, (0,), "sib")
    rank_got()
    total = jnp.zeros(rank_out.shape, jnp.float32)
    for e in range(8):
        total = total + jnp.where(e == q, part, rank_in[e])
    rank = total.T.astype(jnp.bfloat16)
    locals_["base"].wait()
    locals_["up"].wait()
    update = jnp.dot(rank, up_v[adapter], preferred_element_type=jnp.float32)
    query = (base_v[...].astype(jnp.float32) + ADAPTER_SCALING * update).astype(jnp.bfloat16)
    for h in range(8):
        qs[h * 128 : (h + 1) * 128, :] = query[:, h * 128 : (h + 1) * 128]

    peak[...] = jnp.full(peak.shape, LOW, jnp.float32)
    acc[...] = jnp.zeros(acc.shape, jnp.float32)
    scale = HD**-0.5 * LOG2E
    own_key = cont_0[0, 0, 0, 0:1, :]

    row_no = lax.broadcasted_iota(jnp.int32, (128, 128), 0).astype(jnp.float32)

    def fill(n, block, rows):
        at = slice(n * 128, (n + 1) * 128)
        seen = row_no < rows
        kc[at, :] = jnp.where(seen, block[0], own_key)
        vc[at, :128] = jnp.where(seen, block[1], jnp.bfloat16(0))
        vc[at, 128:] = jnp.where(seen, jnp.bfloat16(1), jnp.bfloat16(0))

    def attend(size, mask=None, tiles=range(1024 // ROWS)):
        keys = kc[:size, :]
        values = vc[:size, :]

        def scores(t):
            rows = slice(t * ROWS, (t + 1) * ROWS)
            s = lax.dot_general(
                qs[rows, :], keys, (((1,), (1,)), ((), ())), preferred_element_type=jnp.float32
            )
            if mask is not None:
                s = jnp.concatenate([s[:, :-512], jnp.where(mask, s[:, -512:], LOW)], axis=1)
            return s

        later = scores(tiles[0])
        for t in tiles:
            rows = slice(t * ROWS, (t + 1) * ROWS)
            s = later
            if t + 1 in tiles:
                later = scores(t + 1)
            old = peak[rows, 0:1]
            new = jnp.maximum(old, jnp.max(s, axis=1, keepdims=True))
            w = jnp.exp2((s - new) * scale).astype(jnp.bfloat16)
            factor = jnp.exp2((old - new) * scale)
            acc[rows, :] = acc[rows, :] * factor + jnp.dot(
                w, values, preferred_element_type=jnp.float32
            )
            peak[rows, :] = jnp.broadcast_to(new, (ROWS, 128))

    def plane(k, between):
        for n in range(8):
            i, j, slot = n // 4, n // 2 % 2, n % 2
            fill(n, main[k][i, j, slot], nval[slot, pl.ds(device_of(k, i, j), 1), :])
        for n in range(4):
            fill(8 + n, cont[k][n // 2, n % 2], 128.0 if k == 0 else jnp.where(x + k >= 4, 128.0, 0.0))
        mask = None
        if k == 0:
            lane = lax.broadcasted_iota(jnp.int32, (ROWS, 128), 1)
            token = lax.broadcasted_iota(jnp.int32, (ROWS, 128), 0) + p * 128
            mask = jnp.concatenate(
                [lane + device_of(0, n // 2, n % 2) * 128 <= token for n in range(4)], axis=1
            )
        half = 512 // ROWS
        attend(1536, mask, range(half))
        between()
        attend(1536, mask, range(half, 2 * half))

    def start_writes():
        got("c_ms", "c_pps", "c_mms")
        locals_["wslots"].wait()

        def write_step(b, block):
            local = wslots[r, b] - p * 20
            return jnp.where((local >= 0) & (local < 20), b, block)

        block = lax.fori_loop(0, 16, write_step, jnp.int32(0), unroll=4)
        i, j = (block + c) % 2, (block // 2 + zl) % 2
        away = (block // 4 + 4 - x) % 4
        chosen = cont_0[i, j]
        for k in range(1, 4):
            chosen = jnp.where(away == k, cont[k][i, j], chosen)
        wmine[...] = chosen
        for e in range(1, 4):
            pl.when(e > r)(functools.partial(pl.semaphore_wait, here_req.at[e], 1))
        spread_writes = spread(
            r, wmine, wblk, (write_ssem, write_rsem), [f"r{e}" for e in range(4)]
        )
        spread_writes[0]()
        return spread_writes

    got("c_p")
    send("c_pp", cont, 3, (0, 0), "xp")
    send("c_ps", cont, 3, (0,), "sib")
    got("c_m")
    send("c_mm", cont, 1, (0, 1), "xm")
    send("c_ms", cont, 1, (0,), "sib")

    got("m_z", "m_s")
    send("m_zs", main, 0, (0, 1), "sib")
    got("c_s", "m_zs")
    plane(0, lambda: None)

    got("c_pp")
    send("c_pps", cont, 2, (0, 0), "sib")
    got("c_mm")
    send("c_mms", cont, 2, (0, 1), "sib")
    got("m_pz", "m_mz")
    send("m_pzs", main, 3, (0, 1), "sib")
    send("m_mzs", main, 1, (0, 1), "sib")
    got("m_pp")
    send("m_ppz", main, 2, (0, 0, 0), "zp")
    send("m_pps", main, 2, (0, 0, 0), "sib")
    got("m_mm")
    send("m_mmz", main, 2, (0, 0, 1), "zp")
    send("m_mms", main, 2, (0, 0, 1), "sib")
    got("m_ps", "m_pzs", "c_ps")
    held = []
    plane(3, lambda: held.append(start_writes()))
    write_send, write_got, write_sent = held[0]

    got("o_p")
    send("o_pp", over, 3, (0, 0), "xp")
    send("o_ps", over, 3, (0,), "sib")
    got("o_m")
    send("o_mm", over, 1, (0, 1), "xm")
    send("o_ms", over, 1, (0,), "sib")
    got("m_ppz", "m_mmz")
    send("m_zzs", main, 2, (0, 1), "sib")
    got("m_ms", "m_mzs")
    plane(1, lambda: None)

    def last_hop():
        got("o_pp")
        send("o_pps", over, 2, (0, 0), "sib")
        got("o_mm")
        send("o_mms", over, 2, (0, 1), "sib")

    got("m_pps", "m_mms", "m_zzs")
    plane(2, last_hop)
    got("o_s", "o_ps", "o_ms", "o_pps", "o_mms")
    list_copy.wait()
    for n in range(16):
        name = listed[0, n]
        d = name // 2
        away, i, j = (d // 4 + 4 - x) % 4, (d + c) % 2, (d // 2 + zl) % 2
        fill(n, over_all[away, i, j, name % 2], listed[1, n].astype(jnp.float32))
    attend(2048)

    write_got()
    for e in range(4):
        writes[e] = jnp.where(e == r, wmine[...], wblk[e])

    token = p * 128 + lax.broadcasted_iota(jnp.int32, (128, 128), 0)
    locals_["slens"].wait()
    live = token < slens[r]
    for h in range(8):
        rows = slice(h * 128, (h + 1) * 128)
        value = acc[rows, :128] / acc[rows, 128:]
        out[0, :, rows] = jnp.where(live, value, 0.0).astype(jnp.bfloat16)

    for copy in copies.values():
        copy.wait_send()
    rank_sent()
    write_sent()


def place(wslots, attended_in, writes, pool, attended, pool_after, held, blocks, written, in_sem, out_sem):
    p = lax.axis_index("pool")
    arrivals = [
        pltpu.make_async_copy(src, dst, in_sem.at[n])
        for n, (src, dst) in enumerate(((pool, blocks), (attended_in, held), (writes, written)))
    ]
    for copy in arrivals:
        copy.start()

    def find(tenant):
        def step(b, slot):
            local = wslots[tenant, b] - p * 20
            return jnp.where((local >= 0) & (local < 20), local, slot)

        return lax.fori_loop(0, 16, step, jnp.int32(0), unroll=4)

    slots = [find(tenant) for tenant in range(4)]
    arrivals[1].wait()
    second = pltpu.make_async_copy(held, attended, out_sem.at[0])
    second.start()
    arrivals[2].wait()
    arrivals[0].wait()
    for tenant, slot in enumerate(slots):
        blocks[slot] = written[tenant]
    last = pltpu.make_async_copy(blocks, pool_after, out_sem.at[1])
    last.start()
    second.wait()
    last.wait()


def local(hidden, base, suffix, pool, down, up, table, plens, slens, adapters, wslots):
    bf, f32 = jnp.bfloat16, jnp.float32
    down = down.transpose(0, 2, 1)
    hbm = pl.BlockSpec(memory_space=pltpu.HBM)
    vmem = pl.BlockSpec(memory_space=pltpu.VMEM)
    block = (2, 128, 128)
    attended, writes = pl.pallas_call(
        kernel,
        out_shape=(
            jax.ShapeDtypeStruct(base.shape, bf),
            jax.ShapeDtypeStruct((4,) + block, bf),
        ),
        in_specs=[hbm] * 11,
        out_specs=(vmem, vmem),
        scratch_shapes=[
            *[pltpu.SMEM(a.shape, jnp.int32) for a in (table, plens, slens, adapters, wslots)],
            pltpu.VMEM(pool.shape, bf),
            pltpu.VMEM(hidden.shape[1:], bf),
            pltpu.VMEM(base.shape[1:], bf),
            pltpu.VMEM(down.shape, bf),
            pltpu.VMEM(up.shape, bf),
            *[pltpu.VMEM((2, 2, 2) + block, bf)] * 4,
            pltpu.VMEM((4, 2, 2, 2) + block, bf),
            *[pltpu.VMEM((2, 2) + block, bf)] * 4,
            pltpu.VMEM((4,) + block, bf),
            pltpu.VMEM(block, bf),
            pltpu.VMEM((16, 128), f32),
            pltpu.VMEM((8, 16, 128), f32),
            pltpu.VMEM((1024, 128), bf),
            pltpu.VMEM((1024, 128), f32),
            pltpu.VMEM((1024, 256), f32),
            pltpu.VMEM((2048, 128), bf),
            pltpu.VMEM((2048, 256), bf),
            pltpu.VMEM(table.shape, jnp.int32),
            pltpu.VMEM((4, 16, 128), f32),
            pltpu.VMEM((8, 128), jnp.int32),
            pltpu.SMEM((8, 128), jnp.int32),
            pltpu.SemaphoreType.DMA((13,)),
            pltpu.SemaphoreType.DMA((COPIES,)),
            pltpu.SemaphoreType.DMA((COPIES,)),
            pltpu.SemaphoreType.DMA((8,)),
            pltpu.SemaphoreType.DMA((8,)),
            pltpu.SemaphoreType.DMA((4,)),
            pltpu.SemaphoreType.DMA((4,)),
            pltpu.SemaphoreType.REGULAR((8,)),
            pltpu.SemaphoreType.REGULAR((4,)),
        ],
        compiler_params=pltpu.CompilerParams(
            collective_id=0, has_side_effects=True, vmem_limit_bytes=62 << 20
        ),
        name="attend_all",
    )(table, plens, slens, adapters, wslots, hidden, base, suffix, pool, down, up)
    return pl.pallas_call(
        place,
        out_shape=(
            jax.ShapeDtypeStruct(base.shape, bf),
            jax.ShapeDtypeStruct(pool.shape, bf),
        ),
        in_specs=[pl.BlockSpec(memory_space=pltpu.SMEM)] + [hbm] * 3,
        out_specs=(hbm, hbm),
        scratch_shapes=[
            pltpu.VMEM(base.shape, bf),
            pltpu.VMEM(pool.shape, bf),
            pltpu.VMEM(writes.shape, bf),
            pltpu.SemaphoreType.DMA((3,)),
            pltpu.SemaphoreType.DMA((2,)),
        ],
        compiler_params=pltpu.CompilerParams(vmem_limit_bytes=62 << 20),
        name="place",
    )(wslots, attended, writes, pool)


def solution(mesh):
    in_specs = (
        P("req", "pool", "tp"),
        P("req", "pool", "tp"),
        P("req", None, "pool", "tp"),
        P("pool", None, None, "tp"),
        P(None, "tp", None),
        P(None, None, "tp"),
        P(),
        P(),
        P(),
        P(),
        P(),
    )
    out_specs = (P("req", "pool", "tp"), P("pool", None, None, "tp"))
    return jax.shard_map(local, mesh=mesh, in_specs=in_specs, out_specs=out_specs, check_vma=False)
```

```python
import functools

import jax
import jax.numpy as jnp
from jax import lax
from jax.experimental import pallas as pl
from jax.experimental.pallas import tpu as pltpu
from jax.sharding import PartitionSpec as P

MESH = pl.DeviceIdType.MESH
HD = 128
ADAPTER_SCALING = 0.5
LOG2E = 1.4426950408889634
LOW = -1e30
ROWS = 128
NEAR = ("sib", "xp", "xm", "zp")
ALONG_TP = (0, 1, 7, 2, 6, 3, 5, 4)
COPIES = 38


def kernel(
    table_in, plens_in, slens_in, adapters_in, wslots_in,
    hidden, base, suffix, pool, down, up,
    out, writes,
    table, plens, slens, adapters, wslots,
    pool_v, hid_v, base_v, down_v, up_v,
    main_0, main_1, main_2, main_3, over_all, cont_0, cont_1, cont_2, cont_3,
    wblk, wmine,
    rank_out, rank_in, qs, peak, acc, kc, vc, lines, nval, list_v, listed,
    local_sem, send_sem, recv_sem, rank_ssem, rank_rsem, write_ssem, write_rsem, here_tp, here_req,
):
    p = lax.axis_index("pool")
    y = lax.axis_index("tp")
    r = lax.axis_index("req")
    x, zl, c = p // 4, (p // 2) % 2, p % 2
    x1, x3 = (x + 1) % 4, (x + 3) % 4
    q = jnp.where(y == 0, 0, jnp.where(y <= 4, 2 * y - 1, 16 - 2 * y))
    partner = {
        "sib": {"pool": p + 1 - 2 * c},
        "xp": {"pool": x1 * 4 + zl * 2 + c},
        "xm": {"pool": x3 * 4 + zl * 2 + c},
        "zp": {"pool": p + 2 - 4 * zl},
        **{f"y{e}": {"tp": ALONG_TP[e]} for e in range(8)},
        **{f"r{e}": {"req": e} for e in range(4)},
    }

    main = (main_0, main_1, main_2, main_3)
    over = [over_all.at[k] for k in range(4)]
    cont = (cont_0, cont_1, cont_2, cont_3)

    def device_of(k, i, j):
        return (x + k) % 4 * 4 + (zl + j - 2 * zl * j) * 2 + c + i - 2 * c * i

    locals_ = {}
    for i, (name, src, dst) in enumerate((
        ("table", table_in, table),
        ("suffix", suffix.at[0], cont_0.at[0, 0]),
        ("pool", pool, pool_v),
        ("adapters", adapters_in, adapters),
        ("hidden", hidden.at[0], hid_v),
        ("down", down, down_v),
        ("base", base.at[0], base_v),
        ("up", up, up_v),
        ("plens", plens_in, plens),
        ("lines", table_in, lines),
        ("slens", slens_in, slens),
        ("wslots", wslots_in, wslots),
    )):
        locals_[name] = pltpu.make_async_copy(src, dst, local_sem.at[i])
        locals_[name].start()

    barrier = pltpu.get_barrier_semaphore()

    def signal(sem, to):
        pl.semaphore_signal(sem, inc=1, device_id=partner[to], device_id_type=MESH)

    for name in NEAR:
        signal(barrier, name)
    for e in range(1, 8):
        pl.when(e > q)(functools.partial(signal, barrier, f"y{e}"))
    for e in range(1, 4):
        pl.when(e > r)(functools.partial(signal, barrier, f"r{e}"))
    pl.semaphore_wait(barrier, len(NEAR) + q + r)
    for e in range(7):
        pl.when(e < q)(functools.partial(signal, here_tp.at[q], f"y{e}"))
    for e in range(3):
        pl.when(e < r)(functools.partial(signal, here_req.at[r], f"r{e}"))

    copies = {}

    def send_to(name, src, dst, to):
        i = len(copies)
        copy = pltpu.make_async_remote_copy(
            src_ref=src, dst_ref=dst,
            send_sem=send_sem.at[i], recv_sem=recv_sem.at[i],
            device_id=partner[to], device_id_type=MESH,
        )
        copies[name] = copy
        copy.start()

    def spread(mine, src, place, sems, names):
        there = [
            pltpu.make_async_remote_copy(
                src_ref=src, dst_ref=place.at[mine],
                send_sem=sems[0].at[e], recv_sem=sems[1].at[mine],
                device_id=partner[name], device_id_type=MESH,
            )
            for e, name in enumerate(names)
        ]
        here = [
            pltpu.make_async_remote_copy(
                src_ref=src, dst_ref=place.at[e],
                send_sem=sems[0].at[e], recv_sem=sems[1].at[e],
                device_id=partner[name], device_id_type=MESH,
            )
            for e, name in enumerate(names)
        ]

        def each(what, copies_):
            for e in range(len(names)):
                pl.when(e != mine)(getattr(copies_[e], what))

        return functools.partial(each, "start", there), functools.partial(each, "wait_recv", here), functools.partial(each, "wait_send", there)

    def send(name, buf, k, at, to):
        there = (k + {"xp": 3, "xm": 1}.get(to, 0)) % 4
        place = list(at)
        if to == "sib":
            place[0] = 1 - at[0]
        if to == "zp":
            place[1] = 1 - at[1]
        send_to(name, buf[k].at[at], buf[there].at[tuple(place)], to)

    def got(*names):
        for name in names:
            copies[name].wait_recv()

    locals_["suffix"].wait()
    send("c_z", cont, 0, (0, 0), "zp")

    def own_slots(tenant):
        def step(b, carry):
            count, picks = carry
            local = table[tenant, b] - p * 20
            owned = (local >= 0) & (local < 20)
            picks = tuple(
                jnp.where(owned & (count == k), local, pick) for k, pick in enumerate(picks)
            )
            return count + owned.astype(jnp.int32), picks

        zero = jnp.int32(0)
        return lax.fori_loop(0, 32, step, (zero, (zero,) * 4), unroll=4)[1]

    locals_["table"].wait()
    mine = own_slots(r)
    locals_["pool"].wait()
    for k in range(2):
        main_0[0, 0, k] = pool_v[mine[k]]
    send("m_p", main, 0, (0, 0), "xp")
    send("m_m", main, 0, (0, 0), "xm")
    for k in range(2):
        over_all[0, 0, 0, k] = pool_v[mine[2 + k]]
    send("o_z", over, 0, (0, 0), "zp")
    send("m_s", main, 0, (0, 0), "sib")

    locals_["hidden"].wait()
    locals_["down"].wait()
    locals_["adapters"].wait()
    adapter = adapters[r]
    part = lax.dot_general(
        down_v[adapter], hid_v[...], (((1,), (1,)), ((), ())), preferred_element_type=jnp.float32
    )
    rank_out[...] = part

    got("c_z")
    send("c_p", cont, 0, (0,), "xp")
    send("c_m", cont, 0, (0,), "xm")
    send("c_s", cont, 0, (0,), "sib")
    send("m_z", main, 0, (0, 0), "zp")
    for e in range(1, 8):
        pl.when(e > q)(functools.partial(pl.semaphore_wait, here_tp.at[e], 1))
    rank_send, rank_got, rank_sent = spread(
        q, rank_out, rank_in, (rank_ssem, rank_rsem), [f"y{e}" for e in range(8)]
    )
    rank_send()

    locals_["plens"].wait()
    locals_["lines"].wait()
    device = lax.broadcasted_iota(jnp.int32, (16, 32), 0) * 20
    line = lines[pl.ds(r, 1), :]
    owned = ((line >= device) & (line < device + 20)).astype(jnp.float32)
    before = lax.broadcasted_iota(jnp.int32, (32, 32), 0) < lax.broadcasted_iota(jnp.int32, (32, 32), 1)
    order = jnp.dot(
        owned.astype(jnp.bfloat16), before.astype(jnp.bfloat16), preferred_element_type=jnp.float32
    )
    rest = (plens[r] - lax.broadcasted_iota(jnp.int32, (16, 32), 1) * 128).astype(jnp.float32)
    for k in range(4):
        rows = jnp.sum(jnp.where(order == k, owned * rest, 0.0), axis=1, keepdims=True)
        nval[k] = jnp.broadcast_to(rows, (16, 128))
    more = jnp.maximum(jnp.sum(owned, axis=1, keepdims=True) - 2.0, 0.0)
    more = jnp.broadcast_to(more, (16, 128))
    above = lax.broadcasted_iota(jnp.int32, (16, 16), 1) < lax.broadcasted_iota(jnp.int32, (16, 16), 0)
    ahead = jnp.dot(
        above.astype(jnp.bfloat16), more.astype(jnp.bfloat16), preferred_element_type=jnp.float32
    )
    lane = lax.broadcasted_iota(jnp.int32, (16, 128), 1).astype(jnp.float32)
    number = lax.broadcasted_iota(jnp.int32, (16, 128), 0).astype(jnp.float32)
    third = jnp.where((more > 0.5) & (ahead == lane), 1.0, 0.0)
    fourth = jnp.where((more > 1.5) & (ahead + 1.0 == lane), 1.0, 0.0)
    names = jnp.sum(third * (2.0 * number) + fourth * (2.0 * number + 1.0), axis=0, keepdims=True)
    rows = jnp.sum(third * nval[2] + fourth * nval[3], axis=0, keepdims=True)
    list_v[...] = jnp.zeros(list_v.shape, jnp.int32)
    list_v[0:1, :] = names.astype(jnp.int32)
    list_v[1:2, :] = rows.astype(jnp.int32)
    list_copy = pltpu.make_async_copy(list_v, listed, local_sem.at[12])
    list_copy.start()

    got("m_p")
    send("m_pp", main, 3, (0, 0, 0), "xp")
    send("m_pz", main, 3, (0, 0), "zp")
    send("m_ps", main, 3, (0, 0), "sib")
    got("m_m")
    send("m_mm", main, 1, (0, 0, 1), "xm")
    send("m_mz", main, 1, (0, 0), "zp")
    send("m_ms", main, 1, (0, 0), "sib")
    got("o_z")
    send("o_p", over, 0, (0,), "xp")
    send("o_m", over, 0, (0,), "xm")
    send("o_s", over, 0, (0,), "sib")
    rank_got()
    total = jnp.zeros(rank_out.shape, jnp.float32)
    for e in range(8):
        total = total + jnp.where(e == q, part, rank_in[e])
    rank = total.T.astype(jnp.bfloat16)
    locals_["base"].wait()
    locals_["up"].wait()
    update = jnp.dot(rank, up_v[adapter], preferred_element_type=jnp.float32)
    query = (base_v[...].astype(jnp.float32) + ADAPTER_SCALING * update).astype(jnp.bfloat16)
    for h in range(8):
        qs[h * 128 : (h + 1) * 128, :] = query[:, h * 128 : (h + 1) * 128]

    peak[...] = jnp.full(peak.shape, LOW, jnp.float32)
    acc[...] = jnp.zeros(acc.shape, jnp.float32)
    scale = HD**-0.5 * LOG2E
    own_key = cont_0[0, 0, 0, 0:1, :]

    row_no = lax.broadcasted_iota(jnp.int32, (128, 128), 0).astype(jnp.float32)

    def fill(n, block, rows):
        at = slice(n * 128, (n + 1) * 128)
        seen = row_no < rows
        kc[at, :] = jnp.where(seen, block[0], own_key)
        vc[at, :128] = jnp.where(seen, block[1], jnp.bfloat16(0))
        vc[at, 128:] = jnp.where(seen, jnp.bfloat16(1), jnp.bfloat16(0))

    def attend(size, mask=None, tiles=range(1024 // ROWS)):
        keys = kc[:size, :]
        values = vc[:size, :]

        def scores(t):
            rows = slice(t * ROWS, (t + 1) * ROWS)
            s = lax.dot_general(
                qs[rows, :], keys, (((1,), (1,)), ((), ())), preferred_element_type=jnp.float32
            )
            if mask is not None:
                s = jnp.concatenate([s[:, :-512], jnp.where(mask, s[:, -512:], LOW)], axis=1)
            return s

        later = scores(tiles[0])
        for t in tiles:
            rows = slice(t * ROWS, (t + 1) * ROWS)
            s = later
            if t + 1 in tiles:
                later = scores(t + 1)
            old = peak[rows, 0:1]
            new = jnp.maximum(old, jnp.max(s, axis=1, keepdims=True))
            w = jnp.exp2((s - new) * scale).astype(jnp.bfloat16)
            factor = jnp.exp2((old - new) * scale)
            acc[rows, :] = acc[rows, :] * factor + jnp.dot(
                w, values, preferred_element_type=jnp.float32
            )
            peak[rows, :] = jnp.broadcast_to(new, (ROWS, 128))

    def plane(k, between):
        for n in range(8):
            i, j, slot = n // 4, n // 2 % 2, n % 2
            fill(n, main[k][i, j, slot], nval[slot, pl.ds(device_of(k, i, j), 1), :])
        for n in range(4):
            fill(8 + n, cont[k][n // 2, n % 2], 128.0 if k == 0 else jnp.where(x + k >= 4, 128.0, 0.0))
        mask = None
        if k == 0:
            lane = lax.broadcasted_iota(jnp.int32, (ROWS, 128), 1)
            token = lax.broadcasted_iota(jnp.int32, (ROWS, 128), 0) + p * 128
            mask = jnp.concatenate(
                [lane + device_of(0, n // 2, n % 2) * 128 <= token for n in range(4)], axis=1
            )
        half = 512 // ROWS
        attend(1536, mask, range(half))
        between()
        attend(1536, mask, range(half, 2 * half))

    def start_writes():
        got("c_ms", "c_pps", "c_mms")
        locals_["wslots"].wait()

        def write_step(b, block):
            local = wslots[r, b] - p * 20
            return jnp.where((local >= 0) & (local < 20), b, block)

        block = lax.fori_loop(0, 16, write_step, jnp.int32(0), unroll=4)
        i, j = (block + c) % 2, (block // 2 + zl) % 2
        away = (block // 4 + 4 - x) % 4
        chosen = cont_0[i, j]
        for k in range(1, 4):
            chosen = jnp.where(away == k, cont[k][i, j], chosen)
        wmine[...] = chosen
        for e in range(1, 4):
            pl.when(e > r)(functools.partial(pl.semaphore_wait, here_req.at[e], 1))
        spread_writes = spread(
            r, wmine, wblk, (write_ssem, write_rsem), [f"r{e}" for e in range(4)]
        )
        spread_writes[0]()
        return spread_writes

    got("c_p")
    send("c_pp", cont, 3, (0, 0), "xp")
    send("c_ps", cont, 3, (0,), "sib")
    got("c_m")
    send("c_mm", cont, 1, (0, 1), "xm")
    send("c_ms", cont, 1, (0,), "sib")

    got("m_z", "m_s")
    send("m_zs", main, 0, (0, 1), "sib")
    got("c_s", "m_zs")
    def second_hop():
        got("c_pp")
        send("c_pps", cont, 2, (0, 0), "sib")
        got("c_mm")
        send("c_mms", cont, 2, (0, 1), "sib")

    plane(0, second_hop)

    got("m_pz", "m_mz")
    send("m_pzs", main, 3, (0, 1), "sib")
    send("m_mzs", main, 1, (0, 1), "sib")
    got("m_pp")
    send("m_ppz", main, 2, (0, 0, 0), "zp")
    send("m_pps", main, 2, (0, 0, 0), "sib")
    got("m_mm")
    send("m_mmz", main, 2, (0, 0, 1), "zp")
    send("m_mms", main, 2, (0, 0, 1), "sib")
    got("m_ps", "m_pzs", "c_ps")
    write_send, write_got, write_sent = start_writes()
    plane(3, lambda: None)

    got("o_p")
    send("o_pp", over, 3, (0, 0), "xp")
    send("o_ps", over, 3, (0,), "sib")
    got("o_m")
    send("o_mm", over, 1, (0, 1), "xm")
    send("o_ms", over, 1, (0,), "sib")
    got("m_ppz", "m_mmz")
    send("m_zzs", main, 2, (0, 1), "sib")
    got("m_ms", "m_mzs")
    plane(1, lambda: None)

    def last_hop():
        got("o_pp")
        send("o_pps", over, 2, (0, 0), "sib")
        got("o_mm")
        send("o_mms", over, 2, (0, 1), "sib")

    got("m_pps", "m_mms", "m_zzs")
    plane(2, last_hop)
    got("o_s", "o_ps", "o_ms", "o_pps", "o_mms")
    list_copy.wait()
    for n in range(16):
        name = listed[0, n]
        d = name // 2
        away, i, j = (d // 4 + 4 - x) % 4, (d + c) % 2, (d // 2 + zl) % 2
        fill(n, over_all[away, i, j, name % 2], listed[1, n].astype(jnp.float32))
    attend(2048)

    write_got()
    for e in range(4):
        writes[e] = jnp.where(e == r, wmine[...], wblk[e])

    token = p * 128 + lax.broadcasted_iota(jnp.int32, (128, 128), 0)
    locals_["slens"].wait()
    live = token < slens[r]
    for h in range(8):
        rows = slice(h * 128, (h + 1) * 128)
        value = acc[rows, :128] / acc[rows, 128:]
        out[0, :, rows] = jnp.where(live, value, 0.0).astype(jnp.bfloat16)

    for copy in copies.values():
        copy.wait_send()
    rank_sent()
    write_sent()


def place(wslots, attended_in, writes, pool, attended, pool_after, held, blocks, written, in_sem, out_sem):
    p = lax.axis_index("pool")
    arrivals = [
        pltpu.make_async_copy(src, dst, in_sem.at[n])
        for n, (src, dst) in enumerate(((pool, blocks), (attended_in, held), (writes, written)))
    ]
    for copy in arrivals:
        copy.start()

    def find(tenant):
        def step(b, slot):
            local = wslots[tenant, b] - p * 20
            return jnp.where((local >= 0) & (local < 20), local, slot)

        return lax.fori_loop(0, 16, step, jnp.int32(0), unroll=4)

    slots = [find(tenant) for tenant in range(4)]
    arrivals[1].wait()
    second = pltpu.make_async_copy(held, attended, out_sem.at[0])
    second.start()
    arrivals[2].wait()
    arrivals[0].wait()
    for tenant, slot in enumerate(slots):
        blocks[slot] = written[tenant]
    last = pltpu.make_async_copy(blocks, pool_after, out_sem.at[1])
    last.start()
    second.wait()
    last.wait()


def local(hidden, base, suffix, pool, down, up, table, plens, slens, adapters, wslots):
    bf, f32 = jnp.bfloat16, jnp.float32
    down = down.transpose(0, 2, 1)
    hbm = pl.BlockSpec(memory_space=pltpu.HBM)
    vmem = pl.BlockSpec(memory_space=pltpu.VMEM)
    block = (2, 128, 128)
    attended, writes = pl.pallas_call(
        kernel,
        out_shape=(
            jax.ShapeDtypeStruct(base.shape, bf),
            jax.ShapeDtypeStruct((4,) + block, bf),
        ),
        in_specs=[hbm] * 11,
        out_specs=(vmem, vmem),
        scratch_shapes=[
            *[pltpu.SMEM(a.shape, jnp.int32) for a in (table, plens, slens, adapters, wslots)],
            pltpu.VMEM(pool.shape, bf),
            pltpu.VMEM(hidden.shape[1:], bf),
            pltpu.VMEM(base.shape[1:], bf),
            pltpu.VMEM(down.shape, bf),
            pltpu.VMEM(up.shape, bf),
            *[pltpu.VMEM((2, 2, 2) + block, bf)] * 4,
            pltpu.VMEM((4, 2, 2, 2) + block, bf),
            *[pltpu.VMEM((2, 2) + block, bf)] * 4,
            pltpu.VMEM((4,) + block, bf),
            pltpu.VMEM(block, bf),
            pltpu.VMEM((16, 128), f32),
            pltpu.VMEM((8, 16, 128), f32),
            pltpu.VMEM((1024, 128), bf),
            pltpu.VMEM((1024, 128), f32),
            pltpu.VMEM((1024, 256), f32),
            pltpu.VMEM((2048, 128), bf),
            pltpu.VMEM((2048, 256), bf),
            pltpu.VMEM(table.shape, jnp.int32),
            pltpu.VMEM((4, 16, 128), f32),
            pltpu.VMEM((8, 128), jnp.int32),
            pltpu.SMEM((8, 128), jnp.int32),
            pltpu.SemaphoreType.DMA((13,)),
            pltpu.SemaphoreType.DMA((COPIES,)),
            pltpu.SemaphoreType.DMA((COPIES,)),
            pltpu.SemaphoreType.DMA((8,)),
            pltpu.SemaphoreType.DMA((8,)),
            pltpu.SemaphoreType.DMA((4,)),
            pltpu.SemaphoreType.DMA((4,)),
            pltpu.SemaphoreType.REGULAR((8,)),
            pltpu.SemaphoreType.REGULAR((4,)),
        ],
        compiler_params=pltpu.CompilerParams(
            collective_id=0, has_side_effects=True, vmem_limit_bytes=62 << 20
        ),
        name="attend_all",
    )(table, plens, slens, adapters, wslots, hidden, base, suffix, pool, down, up)
    return pl.pallas_call(
        place,
        out_shape=(
            jax.ShapeDtypeStruct(base.shape, bf),
            jax.ShapeDtypeStruct(pool.shape, bf),
        ),
        in_specs=[pl.BlockSpec(memory_space=pltpu.SMEM)] + [hbm] * 3,
        out_specs=(hbm, hbm),
        scratch_shapes=[
            pltpu.VMEM(base.shape, bf),
            pltpu.VMEM(pool.shape, bf),
            pltpu.VMEM(writes.shape, bf),
            pltpu.SemaphoreType.DMA((3,)),
            pltpu.SemaphoreType.DMA((2,)),
        ],
        compiler_params=pltpu.CompilerParams(vmem_limit_bytes=62 << 20),
        name="place",
    )(wslots, attended, writes, pool)


def solution(mesh):
    in_specs = (
        P("req", "pool", "tp"),
        P("req", "pool", "tp"),
        P("req", None, "pool", "tp"),
        P("pool", None, None, "tp"),
        P(None, "tp", None),
        P(None, None, "tp"),
        P(),
        P(),
        P(),
        P(),
        P(),
    )
    out_specs = (P("req", "pool", "tp"), P("pool", None, None, "tp"))
    return jax.shard_map(local, mesh=mesh, in_specs=in_specs, out_specs=out_specs, check_vma=False)
```
